128 devices in a mesh: dp: 2 (over core), tensor: 64 (over z, y, x).
Axes of the slice: x: 4, y: 4, z: 4, core: 2. Of those that a mesh axis runs over, the one named last changes fastest.
Arguments:
- activations: bfloat16 [4096, 5120], P(('dp', 'tensor')), may hold values from -7 to 7
- head_grads: bfloat16 [4096, 2048], P('dp', 'tensor'), may hold values from -10 to 10
- momentum: bfloat16 [2, 64, 80, 2048], P('dp', 'tensor'), may hold values from -6 to 6
Outputs:
- new_momentum: bfloat16 [2, 64, 80, 2048], P('dp', 'tensor')
- update: bfloat16 [64, 80, 2048], P('tensor')
The draws below stay inside these ranges and needn't reach their ends.
All inputs are finite; a program needn't handle non-finite values.
Results may differ from the reference program's by a relative error of at most 0.001.
Values may be sent and summed in bfloat16 or wider, within the bound.
A program may use at most 128 MiB of HBM per device.

```python
import math
import jax
import jax.numpy as jnp
from jax import lax

D = 5120
BLOCK = 64
KEEP = 8
KV_COLS = 2048
TOK_REP = 2048
REPLICAS = 2
TOKENS = 4096


def feature_scale():
    position = (jnp.arange(D, dtype=jnp.int32) % BLOCK).astype(jnp.float32)
    return jnp.exp(math.log(3.0) * position / (BLOCK - 1)) / math.sqrt(4.0 / math.log(3.0))


def replica_scale(low, high):
    replica = (jnp.arange(TOKENS, dtype=jnp.int32) // TOK_REP).astype(jnp.float32)
    return low * jnp.exp(math.log(high / low) * replica / max(REPLICAS - 1, 1))


def draw_activations(key, part):
    key = jax.random.fold_in(key, 11)
    base_values = jnp.clip(jax.random.normal(key, (TOKENS, D), jnp.float32), -4.0, 4.0)
    return (base_values * feature_scale()[None, :]).astype(jnp.bfloat16)


def draw_head_grads(key, part):
    key = jax.random.fold_in(key, 7)
    base_key, col_key = jax.random.split(key, 2)
    column = jnp.arange(KV_COLS, dtype=jnp.float32)
    rising = jnp.exp(math.log(3.0) * column / max(KV_COLS - 1, 1))
    spread = jnp.exp(jax.random.uniform(col_key, (KV_COLS,), jnp.float32, 0.0, math.log(10.0)))
    norm_const = math.sqrt(4.0 / math.log(3.0) * 99.0 / (2.0 * math.log(10.0)))
    base_values = jnp.clip(jax.random.normal(base_key, (TOKENS, KV_COLS), jnp.float32), -4.0, 4.0)
    per_replica = replica_scale(0.25, 4.0)
    token_scale = per_replica / (norm_const * math.sqrt(TOK_REP))
    return (base_values * token_scale[:, None] * (rising * spread)[None, :]).astype(jnp.bfloat16)


def shard_levels(own_key, shape, pieces, least, top_value):
    def one(dim, shards_of):
        draws = jax.random.uniform(jax.random.fold_in(jax.random.fold_in(own_key, 6), dim), (shards_of,), jnp.float32, least / len(pieces), top_value / len(pieces))
        return jnp.repeat(jnp.exp(draws), shape[dim] // shards_of).reshape((-1,) + (1,) * (len(shape) - dim - 1))

    level = one(*pieces[0])
    for cut in pieces[1:]:
        level = level * one(*cut)
    return level


def noise(key, shape, width, reach, shards=(), kind=jnp.bfloat16):
    values = jax.random.normal(key, shape, jnp.float32) * width
    if len(shards) > 0:
        values = shard_levels(key, shape, shards, -0.22, 0.18) * values
    return jnp.clip(values, min=-reach, max=reach).astype(kind)


def setup_inputs(seed: int = 0) -> dict:
    keys = jax.random.split(jax.random.key(seed), 4)
    return {
        "activations": draw_activations(jax.random.fold_in(keys[3], 71), 0),
        "head_grads": draw_head_grads(jax.random.fold_in(keys[3], 71), 0),
        "momentum": noise(keys[2], (REPLICAS, BLOCK, D // BLOCK, KV_COLS), 1.0, 6.0, ((0, 2), (1, 64))),
    }


def dct_basis():
    frequency = jnp.arange(KEEP, dtype=jnp.float32)[:, None]
    position = jnp.arange(BLOCK, dtype=jnp.float32)[None, :]
    normalizer = jnp.where(frequency == 0, math.sqrt(1.0 / BLOCK), math.sqrt(2.0 / BLOCK))
    return normalizer * jnp.cos(math.pi * (2.0 * position + 1.0) * frequency / (2.0 * BLOCK))

def forward(values, basis_table):
    row_count, col_count = values.shape
    blocks = values.reshape(row_count // BLOCK, BLOCK, col_count // BLOCK, BLOCK)
    return jnp.einsum('kn,anbm,lm->akbl', basis_table, blocks, basis_table, precision=lax.Precision.HIGHEST)

def inverse(spectrum, basis_table):
    values = jnp.einsum('kn,akbl,lm->anbm', basis_table, spectrum, basis_table, precision=lax.Precision.HIGHEST)
    return values.reshape(spectrum.shape[0] * BLOCK, spectrum.shape[2] * BLOCK)

def to_layout(values):
    return values.reshape(D // BLOCK, BLOCK, KV_COLS).transpose(1, 0, 2)

def reference(activations, head_grads, momentum):
    basis_table = dct_basis()

    def one_replica(replica):
        offset = (replica * TOK_REP).astype(jnp.int32)
        token_rows = lax.dynamic_slice_in_dim(activations, offset, TOK_REP, 0)
        cotangent = lax.dynamic_slice_in_dim(head_grads, offset, TOK_REP, 0)
        gradient = lax.dot_general(token_rows, cotangent, (((0,), (0,)), ((), ())), preferred_element_type=jnp.float32)
        squares = jnp.sum(gradient * gradient)
        root_mean = jnp.sqrt(squares / (D * KV_COLS) + 1e-06)
        factor = jnp.minimum(jnp.float32(1.0), 1.0 / root_mean)
        previous = lax.dynamic_index_in_dim(momentum, replica, 0, keepdims=False)
        previous = previous.astype(jnp.float32).transpose(1, 0, 2).reshape(D, KV_COLS)
        combined = 0.9 * previous + factor * gradient
        spectrum = forward(combined, basis_table)
        residual = combined - inverse(spectrum, basis_table)
        return (to_layout(residual).astype(jnp.bfloat16), spectrum)
    new_momentum, spectra = lax.map(one_replica, jnp.arange(REPLICAS, dtype=jnp.int32))
    averaged = lax.optimization_barrier(jnp.sum(spectra, axis=0)) / REPLICAS
    update = to_layout(inverse(averaged, basis_table)).astype(jnp.bfloat16)
    return (new_momentum, update)
```

```python
import math

import jax
import jax.numpy as jnp
import ml_dtypes
import numpy as np
from jax import lax
from jax.experimental import pallas as pl
from jax.experimental.pallas import tpu as pltpu
from jax.sharding import PartitionSpec as P

BLOCK = 64
KEEP = 8
RBLOCKS = 80
COLS = 2048
TOKENS = 2048
LINE = 4
PLANE = 16
ZCOLS = COLS // LINE
ZTOK = TOKENS // LINE
MESH = pl.DeviceIdType.MESH
F32 = jnp.float32
BF16 = jnp.bfloat16
NT = (((1,), (1,)), ((), ()))
TN = (((0,), (0,)), ((), ()))
NN = (((1,), (0,)), ((), ()))


def split(table):
    high = table.astype(np.float32).astype(ml_dtypes.bfloat16)
    low = (table - high.astype(np.float64)).astype(np.float32).astype(ml_dtypes.bfloat16)
    return high, low


def tables():
    k = np.arange(KEEP)[:, None]
    n = np.arange(BLOCK)[None, :]
    scale = np.where(k == 0, math.sqrt(1.0 / BLOCK), math.sqrt(2.0 / BLOCK))
    basis = scale * np.cos(math.pi * (2 * n + 1) * k / (2 * BLOCK))
    sort = np.zeros((256, 256))
    for a in range(4):
        for z in range(LINE):
            for i in range(PLANE):
                sort[a * 64 + z * 16 + i, i * 16 + z * 4 + a] = 1
    pick = np.zeros((LINE * RBLOCKS, 384))
    for tile in range(RBLOCKS // 4):
        for z in range(LINE):
            for a in range(4):
                pick[z * RBLOCKS + 4 * tile + a, tile * 16 + z * 4 + a] = 1
    across = np.kron(np.eye(8), basis)
    order = np.array([z * PLANE + i for i in range(PLANE) for z in range(LINE)])
    project = np.kron((basis.T @ basis)[np.ix_(order, order)], np.eye(4))
    spread_h, spread_l = split(np.kron(np.eye(4), basis))
    spread = np.concatenate([spread_h, spread_h, spread_l], axis=0)
    return (
        sort.astype(ml_dtypes.bfloat16),
        pick.astype(ml_dtypes.bfloat16),
        np.eye(32).astype(ml_dtypes.bfloat16),
        np.stack(split(across)),
        np.stack(split(project)),
        spread,
    )


def dot(a, b, dims):
    return lax.dot_general(a, b, dims, preferred_element_type=F32)


def parts(x):
    high = x.astype(BF16)
    return high, (x - high.astype(F32)).astype(BF16)


def kernel(
    act, head, mom, sort, pick, eye, across, project, spread,
    new_out, upd_out,
    stack, a_send, a_recv, at, gt, grad, grad_row,
    wm_send, wm_recv, pm_send, pm_recv, qm_send, qm_recv, vm, vm_all,
    wg, pg_send, pg_recv, qg_send, qg_recv, vg, vg_all, total_v,
    sa, ra, sz, rz, sg, rg, sgr, rgr, swm, rwm,
    spm, rpm, sqm, rqm, svm, rvm, spg, rpg, sqg, rqg, svg, rvg,
):
    core = lax.axis_index("dp")
    t = lax.axis_index("tensor")
    z, me = lax.div(t, 16), lax.rem(t, 16)
    y, x = lax.div(me, 4), lax.rem(me, 4)

    def shift(v, by):
        return lax.rem(v + by % 4, 4)

    def inplane(d):
        return shift(y, d // 4) * 4 + shift(x, d % 4)

    def copy(src, dst, ssem, rsem, c, zz, ii):
        return pltpu.make_async_remote_copy(
            src_ref=src, dst_ref=dst, send_sem=ssem, recv_sem=rsem,
            device_id=(c, zz * 16 + ii), device_id_type=MESH,
        )

    sent = []

    def go(c):
        c.start()
        sent.append(c)
        return c

    barrier = pltpu.get_barrier_semaphore()
    partners = [(core, z, inplane(d)) for d in range(1, 16)]
    partners += [(core, shift(z, d), me) for d in range(1, 4)]
    partners += [(1 - core, shift(z, d), me) for d in range(4)]
    for c, zz, ii in partners:
        pl.semaphore_signal(barrier, inc=1, device_id=(c, zz * 16 + ii), device_id_type=MESH)
    pl.semaphore_wait(barrier, len(partners))

    for tile in range(20):
        stack[tile * 32:(tile + 1) * 32, :] = act[:, tile * 256:(tile + 1) * 256]
    sorted_cols = dot(stack[...], sort[...], NN)
    group = lax.broadcasted_iota(jnp.int32, (32, 128), 1) // 16
    zero = jnp.zeros((32, 128), F32)
    for half in range(2):
        for octet in range(3):
            v = []
            for tile in range(octet * 8, octet * 8 + 8):
                if tile < 20:
                    v.append(sorted_cols[tile * 32:(tile + 1) * 32, half * 128:(half + 1) * 128])
                else:
                    v.append(zero)
            for d in (1, 2, 4):
                low = (group // d) % 2 == 0
                for k in range(8):
                    if k & d == 0:
                        a, b = v[k], v[k | d]
                        v[k] = jnp.where(low, a, pltpu.roll(b, 16 * d, 1))
                        v[k | d] = jnp.where(low, pltpu.roll(a, 128 - 16 * d, 1), b)
            for k in range(8):
                a_send[half * 8 + k, :, octet * 128:(octet + 1) * 128] = v[k].astype(BF16)
    a_copies = []
    for d in range(1, 16):
        to = inplane(d)
        a_copies.append(go(copy(a_send.at[to], a_recv.at[me], sa.at[d - 1], ra.at[d - 1], core, z, to)))
    a_recv[me] = a_send[me]

    gt[me] = dot(eye[...], head[...], NT).astype(BF16)

    def near(axis, by):
        if axis == 0:
            return y * 4 + shift(x, by)
        return shift(y, by) * 4 + x

    def near2(half, da, db):
        if half == 0:
            return shift(y, db) * 4 + shift(x, da)
        return shift(y, da) * 4 + shift(x, db)

    def g_copy(half, slot, rows, sem, to):
        lanes = pl.ds(half * 1024, 1024)
        where = gt.at[slot, pl.ds(rows[0], rows[1]), lanes]
        return copy(where, where, sg.at[half, sem], rg.at[half, sem], core, z, to)

    whole, upper, lower = (0, 32), (0, 16), (16, 16)

    for half in range(2):
        go(g_copy(half, me, whole, 0, near2(half, 1, 0)))
        go(g_copy(half, me, whole, 1, near2(half, -1, 0)))
    for half in range(2):
        go(g_copy(half, me, whole, 4, near2(half, 0, 1)))
        go(g_copy(half, me, whole, 5, near2(half, 0, -1)))

    wm_send[...] = jnp.zeros_like(wm_send)
    wg[...] = jnp.zeros_like(wg)
    for zz in range(LINE):
        piece = mom[:, zz * ZCOLS:(zz + 1) * ZCOLS]
        wm_send[zz, :, 0:RBLOCKS] = dot(across[0], piece, NT) + dot(across[1], piece, NT)
    wm_copies = []
    for d in range(1, 4):
        to = shift(z, d)
        wm_copies.append(go(copy(wm_send.at[to], wm_recv.at[z], swm.at[d - 1], rwm.at[d - 1], core, to, me)))
    wm_recv[z] = wm_send[z]

    def g_wait_from(half, da, db, rows, sem, to):
        g_copy(half, near2(half, da, db), rows, sem, to).wait_recv()

    for half in range(2):
        g_wait_from(half, -1, 0, whole, 0, near2(half, 1, 0))
        go(g_copy(half, near2(half, -1, 0), upper, 2, near2(half, 1, 0)))
        g_wait_from(half, 1, 0, whole, 1, near2(half, -1, 0))
        go(g_copy(half, near2(half, 1, 0), lower, 3, near2(half, -1, 0)))
    for half in range(2):
        for j, da in ((1, -1), (2, 1)):
            go(g_copy(half, near2(half, da, 0), whole, 4 + 4 * j, near2(half, 0, 1)))
            go(g_copy(half, near2(half, da, 0), whole, 5 + 4 * j, near2(half, 0, -1)))

    for c in a_copies:
        c.wait_recv()
    at[z] = dot(pick[...], a_recv[...].reshape(ZTOK, 384), NT).astype(BF16)

    def z_copy(slot, rows, sem, to):
        where = at.at[slot, pl.ds(rows[0], rows[1]), :]
        return copy(where, where, sz.at[sem], rz.at[sem], core, to, me)

    every, first, second = (0, 320), (0, 160), (160, 160)
    zu, zd, zo = shift(z, 1), shift(z, -1), shift(z, 2)
    go(z_copy(z, every, 0, zu))
    go(z_copy(z, every, 1, zd))

    def regroup_w(src, dst):
        for q in range(PLANE):
            for zz in range(LINE):
                dst[q, 4 * zz:4 * zz + 4, :] = src[zz, 4 * q:4 * q + 4, :]

    def regroup_v(src, dst):
        for q in range(PLANE):
            for zz in range(LINE):
                dst[zz, 4 * q:4 * q + 4, :] = src[q, 4 * zz:4 * zz + 4, :]

    def plane_start(src, dst, ssem, rsem):
        out = []
        for d in range(1, 16):
            to = inplane(d)
            out.append(go(copy(src.at[to], dst.at[me], ssem.at[d - 1], rsem.at[d - 1], core, z, to)))
        dst[me] = src[me]
        return out

    def line_start(src, dst, ssem, rsem):
        out = []
        for d in range(4):
            to = shift(z, d)
            if d > 0:
                out.append(go(copy(src.at[to], dst.at[core, z], ssem.at[0, d], rsem.at[0, d], core, to, me)))
            out.append(go(copy(src.at[to], dst.at[core, z], ssem.at[1, d], rsem.at[1, d], 1 - core, to, me)))
        dst[core, z] = src[z]
        return out

    def apply_project(w):
        high, low = parts(w)
        return dot(project[0], high, NN) + dot(project[0], low, NN) + dot(project[1], high, NN)

    for c in wm_copies:
        c.wait_recv()
    regroup_w(wm_recv, pm_send)
    pm_copies = plane_start(pm_send, pm_recv, spm, rpm)

    for half in range(2):
        g_wait_from(half, 2, 0, upper, 2, near2(half, 1, 0))
        g_wait_from(half, 2, 0, lower, 3, near2(half, -1, 0))
        go(g_copy(half, near2(half, 2, 0), whole, 16, near2(half, 0, 1)))
        go(g_copy(half, near2(half, 2, 0), whole, 17, near2(half, 0, -1)))
    for j, da in ((0, 0), (1, -1), (2, 1)):
        for half in range(2):
            g_wait_from(half, da, -1, whole, 4 + 4 * j, near2(half, 0, 1))
            go(g_copy(half, near2(half, da, -1), upper, 6 + 4 * j, near2(half, 0, 1)))
            g_wait_from(half, da, 1, whole, 5 + 4 * j, near2(half, 0, -1))
            go(g_copy(half, near2(half, da, 1), lower, 7 + 4 * j, near2(half, 0, -1)))

    for c in pm_copies:
        c.wait_recv()
    qm_send[...] = apply_project(pm_recv[...].reshape(256, 128)).reshape(PLANE, 16, 128)
    qm_copies = plane_start(qm_send, qm_recv, sqm, rqm)

    z_copy(zd, every, 0, zu).wait_recv()
    go(z_copy(zd, first, 2, zu))
    z_copy(zu, every, 1, zd).wait_recv()
    go(z_copy(zu, second, 3, zd))

    for half in range(2):
        g_wait_from(half, 2, -1, whole, 16, near2(half, 0, 1))
        go(g_copy(half, near2(half, 2, -1), upper, 18, near2(half, 0, 1)))
        g_wait_from(half, 2, 1, whole, 17, near2(half, 0, -1))
        go(g_copy(half, near2(half, 2, 1), lower, 19, near2(half, 0, -1)))

    for c in qm_copies:
        c.wait_recv()
    regroup_v(qm_recv, vm)
    vm_copies = line_start(vm, vm_all, svm, rvm)

    for j, da in ((0, 0), (1, -1), (2, 1), (3, 2)):
        for half in range(2):
            g_wait_from(half, da, 2, upper, 6 + 4 * j, near2(half, 0, 1))
            g_wait_from(half, da, 2, lower, 7 + 4 * j, near2(half, 0, -1))
    z_copy(zo, first, 2, zu).wait_recv()
    z_copy(zo, second, 3, zd).wait_recv()

    acc = None
    for zz in range(LINE):
        term = dot(at[zz], gt[:, :, zz * ZTOK:(zz + 1) * ZTOK].reshape(ZCOLS, ZTOK), NT)
        acc = term if acc is None else acc + term
    grad[...] = acc.reshape(LINE, RBLOCKS, ZCOLS)
    grad_copies = []
    for d in range(1, 4):
        to = shift(z, d)
        grad_copies.append(go(copy(grad.at[to], grad_row.at[z], sgr.at[d - 1], rgr.at[d - 1], core, to, me)))
    grad_row[z] = grad[z]
    for zz in range(LINE):
        high, low = parts(grad[zz])
        wg[zz, :, 0:RBLOCKS] = (
            dot(across[0], high, NT) + dot(across[0], low, NT) + dot(across[1], high, NT)
        )
    squares = jnp.zeros((8, 128), F32)
    for zz in range(LINE):
        piece = grad[zz]
        sq = piece * piece
        for lane in range(4):
            squares += jnp.sum(sq[:, lane * 128:(lane + 1) * 128].reshape(10, 8, 128), axis=0)
    regroup_w(wg, pg_send)
    for q in range(PLANE):
        pg_send[q, 16:24, :] = squares
    pg_copies = plane_start(pg_send, pg_recv, spg, rpg)
    for c in pg_copies:
        c.wait_recv()
    qg_send[...] = apply_project(pg_recv[:, 0:16, :].reshape(256, 128)).reshape(PLANE, 16, 128)
    qg_copies = plane_start(qg_send, qg_recv, sqg, rqg)
    plane_sq = jnp.sum(pg_recv[:, 16:24, :], axis=0)
    for zz in range(LINE):
        vg[zz, 64:72, :] = plane_sq
    for c in qg_copies:
        c.wait_recv()
    regroup_v(qg_recv, vg)
    vg_copies = line_start(vg, vg_all, svg, rvg)
    for c in vm_copies:
        c.wait_recv()
    for c in vg_copies:
        c.wait_recv()

    factors = []
    for r in range(2):
        square = vg_all[r, 0, 64:72, :]
        for zz in range(1, LINE):
            square = square + vg_all[r, zz, 64:72, :]
        square = jnp.sum(jnp.sum(square, axis=0, keepdims=True), axis=1, keepdims=True)
        factors.append(jnp.minimum(F32(1.0), 1.0 / jnp.sqrt(square / (RBLOCKS * BLOCK * COLS) + 1e-06)))
        for zz in range(LINE):
            total_v[r, zz * 64:(zz + 1) * 64, :] = (
                F32(0.9) * vm_all[r, zz] + factors[r] * vg_all[r, zz, 0:64, :]
            )
    factor = jnp.where(core == 0, factors[0], factors[1])

    def kept(v):
        high, low = parts(v)
        return dot(jnp.concatenate([high, low, high], axis=0), spread[...], TN)[0:RBLOCKS]

    for g in range(8):
        rows = slice(g * 32, (g + 1) * 32)
        cols = slice(g * 256, (g + 1) * 256)
        both = (total_v[0, rows, :] + total_v[1, rows, :]) * F32(0.5)
        upd_out[:, cols] = kept(both).astype(BF16)
    for c in grad_copies:
        c.wait_recv()
    for g in range(8):
        rows = slice(g * 32, (g + 1) * 32)
        cols = slice(g * 256, (g + 1) * 256)
        local = slice((g % 2) * 256, (g % 2) * 256 + 256)
        full = F32(0.9) * mom[:, cols].astype(F32) + factor * grad_row[g // 2, :, local]
        new_out[:, cols] = (full - kept(total_v[core, rows, :])).astype(BF16)
    for c in sent:
        c.wait_send()


def body(activations, head_grads, momentum):
    dma = pltpu.SemaphoreType.DMA
    consts = [jnp.asarray(c) for c in tables()]
    vmem = pl.BlockSpec(memory_space=pltpu.VMEM)
    scratch = [
        pltpu.VMEM((640, 256), BF16),
        pltpu.VMEM((PLANE, 32, 384), BF16),
        pltpu.VMEM((PLANE, 32, 384), BF16),
        pltpu.VMEM((LINE, 320, ZTOK), BF16),
        pltpu.VMEM((PLANE, 32, TOKENS), BF16),
        pltpu.VMEM((LINE, RBLOCKS, ZCOLS), F32),
        pltpu.VMEM((LINE, RBLOCKS, ZCOLS), F32),
        pltpu.VMEM((LINE, 64, 128), F32),
        pltpu.VMEM((LINE, 64, 128), F32),
        pltpu.VMEM((PLANE, 16, 128), F32),
        pltpu.VMEM((PLANE, 16, 128), F32),
        pltpu.VMEM((PLANE, 16, 128), F32),
        pltpu.VMEM((PLANE, 16, 128), F32),
        pltpu.VMEM((LINE, 64, 128), F32),
        pltpu.VMEM((2, LINE, 64, 128), F32),
        pltpu.VMEM((LINE, 64, 128), F32),
        pltpu.VMEM((PLANE, 24, 128), F32),
        pltpu.VMEM((PLANE, 24, 128), F32),
        pltpu.VMEM((PLANE, 16, 128), F32),
        pltpu.VMEM((PLANE, 16, 128), F32),
        pltpu.VMEM((LINE, 72, 128), F32),
        pltpu.VMEM((2, LINE, 72, 128), F32),
        pltpu.VMEM((2, 256, 128), F32),
    ]
    for shape in ((15,), (4,), (2, 20), (3,), (3,), (15,), (15,), (2, 4), (15,), (15,), (2, 4)):
        scratch += [dma(shape), dma(shape)]
    new, upd = pl.pallas_call(
        kernel,
        out_shape=(
            jax.ShapeDtypeStruct((RBLOCKS, COLS), BF16),
            jax.ShapeDtypeStruct((RBLOCKS, COLS), BF16),
        ),
        in_specs=[vmem] * 9,
        out_specs=(vmem, vmem),
        scratch_shapes=scratch,
        compiler_params=pltpu.CompilerParams(
            collective_id=0, has_side_effects=True, vmem_limit_bytes=40 * 1024 * 1024
        ),
    )(activations, head_grads, momentum.reshape(RBLOCKS, COLS), *consts)
    return new[None, None], upd[None]


def solution(mesh):
    placed = (P(("dp", "tensor"), None), P("dp", "tensor"), P("dp", "tensor", None, None))
    return jax.shard_map(
        body,
        mesh=mesh,
        in_specs=placed,
        out_specs=(P("dp", "tensor", None, None), P("tensor", None, None)),
        check_vma=False,
    )
```

```python
import math

import jax
import jax.numpy as jnp
import ml_dtypes
import numpy as np
from jax import lax
from jax.experimental import pallas as pl
from jax.experimental.pallas import tpu as pltpu
from jax.sharding import PartitionSpec as P

BLOCK = 64
KEEP = 8
RBLOCKS = 80
COLS = 2048
TOKENS = 2048
LINE = 4
PLANE = 16
ZCOLS = COLS // LINE
ZTOK = TOKENS // LINE
MESH = pl.DeviceIdType.MESH
F32 = jnp.float32
BF16 = jnp.bfloat16
NT = (((1,), (1,)), ((), ()))
TN = (((0,), (0,)), ((), ()))
NN = (((1,), (0,)), ((), ()))
ORDER = ("a0", "a1", "a3", "s", "a2", "g0", "z0", "f", "z1", "z3", "g1", "g2", "z2", "g3", "m1")
START = "A12"
MSTEPS = ((2,), (3, 4))
AORD = (1, 3, 2, 4, 12, 5, 7, 13, 15, 6, 14, 8, 9, 11, 10)


def split(table):
    high = table.astype(np.float32).astype(ml_dtypes.bfloat16)
    low = (table - high.astype(np.float64)).astype(np.float32).astype(ml_dtypes.bfloat16)
    return high, low


def tables():
    k = np.arange(KEEP)[:, None]
    n = np.arange(BLOCK)[None, :]
    scale = np.where(k == 0, math.sqrt(1.0 / BLOCK), math.sqrt(2.0 / BLOCK))
    basis = scale * np.cos(math.pi * (2 * n + 1) * k / (2 * BLOCK))
    sort = np.zeros((256, 256))
    for a in range(4):
        for z in range(LINE):
            for i in range(PLANE):
                sort[a * 64 + z * 16 + i, i * 16 + z * 4 + a] = 1
    pick = np.zeros((LINE * RBLOCKS, 384))
    for tile in range(RBLOCKS // 4):
        for z in range(LINE):
            for a in range(4):
                pick[z * RBLOCKS + 4 * tile + a, tile * 16 + z * 4 + a] = 1
    across = np.kron(np.eye(8), basis)
    order = np.array([z * PLANE + i for i in range(PLANE) for z in range(LINE)])
    project = np.kron((basis.T @ basis)[np.ix_(order, order)], np.eye(4))
    gather_n = np.kron(basis[:, order], np.eye(4))
    back = np.zeros((BLOCK, 2, 4, 2, KEEP, 4))
    spread = np.zeros((2, 4, 2, 2, 4, 2, 4, BLOCK))
    for r in range(2):
        for l in range(4):
            back[:, r, l, r, :, l] = basis.T
        for b in range(4):
            for half in range(2):
                rows = basis[half * 4:half * 4 + 4]
                spread[r, b, half, r, :, 0, b] = rows
                spread[:, b, half, r, :, 1, b] = 0.5 * rows
    back_h, back_l = split(back.reshape(512, 64))
    back = np.concatenate([back_h, back_h, back_l], axis=1)
    spread_h, spread_l = split(spread.reshape(2, 64, 512))
    spread = np.concatenate([spread_h, spread_h, spread_l], axis=1)
    return (
        sort.astype(ml_dtypes.bfloat16),
        pick.astype(ml_dtypes.bfloat16),
        np.concatenate(split(across), axis=0),
        np.stack(split(project)),
        np.concatenate(split(gather_n), axis=0),
        back,
        spread,
    )


def dot(a, b, dims):
    return lax.dot_general(a, b, dims, preferred_element_type=F32)


def parts(x):
    high = x.astype(BF16)
    return high, (x - high.astype(F32)).astype(BF16)


def kernel(
    act_hbm, head_hbm, mom_hbm, sort_hbm, pick_hbm, across_hbm, project_hbm, keep_hbm, back_hbm, spread_hbm,
    new_out, upd_out,
    act, mom, sort, pick, across, project, keep, back, spread, stack,
    a_send, a_recv, at, gt, grad, grad_row,
    wm_send, wm_recv, pm_send, pm_recv, qm_send, qm_recv, vm, vm_all,
    wg, pg_send, pg_recv, coef, vg, vg_all, vm_rows, total_v,
    load, sa, ra, sz, rz, sg, rg, sgr, rgr, swm, rwm,
    spm, rpm, sqm, rqm, svm, rvm, spg, rpg, sqg, rqg, sfg, rfg,
):
    core = lax.axis_index("dp")
    t = lax.axis_index("tensor")
    z, me = lax.div(t, 16), lax.rem(t, 16)
    y, x = lax.div(me, 4), lax.rem(me, 4)

    def shift(v, by):
        return lax.rem(v + by % 4, 4)

    def inplane(d):
        return shift(y, d // 4) * 4 + shift(x, d % 4)

    def hops(dz, d):
        return sum(min(v, 4 - v) for v in (dz, d // 4, d % 4))

    far_first = sorted(range(1, 16), key=lambda d: -hops(0, d))

    def copy(src, dst, ssem, rsem, c, zz, ii):
        return pltpu.make_async_remote_copy(
            src_ref=src, dst_ref=dst, send_sem=ssem, recv_sem=rsem,
            device_id=(c, zz * 16 + ii), device_id_type=MESH,
        )

    sent = []
    arrived = set()

    def go(c):
        c.start()
        sent.append(c)
        return c

    def wait(c):
        c.wait_recv()
        arrived.add(id(c))

    barrier = pltpu.get_barrier_semaphore()
    partners = [(core, z, inplane(d)) for d in far_first]
    partners += [(core, shift(z, d), me) for d in (2, 1, 3)] + [(1 - core, z, me)]
    for c, zz, ii in partners:
        pl.semaphore_signal(barrier, inc=1, device_id=(c, zz * 16 + ii), device_id_type=MESH)

    loads = {}
    for k, (name, src, dst) in enumerate((
        ("act", act_hbm, act), ("sort", sort_hbm, sort), ("head", head_hbm, gt.at[me]),
        ("mom", mom_hbm, mom), ("pick", pick_hbm, pick), ("across", across_hbm, across),
        ("project", project_hbm, project), ("keep", keep_hbm, keep), ("back", back_hbm, back), ("spread", spread_hbm, spread),
    )):
        loads[name] = pltpu.make_async_copy(src, dst, load.at[k])
        loads[name].start()

    loads["act"].wait()
    loads["sort"].wait()
    for tile in range(20):
        stack[tile * 32:(tile + 1) * 32, :] = act[:, tile * 256:(tile + 1) * 256]
    sorted_cols = dot(stack[...], sort[...], NN)
    group = lax.broadcasted_iota(jnp.int32, (32, 128), 1) // 16
    zero = jnp.zeros((32, 128), F32)
    for half in range(2):
        for octet in range(3):
            v = []
            for tile in range(octet * 8, octet * 8 + 8):
                if tile < 20:
                    v.append(sorted_cols[tile * 32:(tile + 1) * 32, half * 128:(half + 1) * 128])
                else:
                    v.append(zero)
            for d in (1, 2, 4):
                low = (group // d) % 2 == 0
                for k in range(8):
                    if k & d == 0:
                        a, b = v[k], v[k | d]
                        v[k] = jnp.where(low, a, pltpu.roll(b, 16 * d, 1))
                        v[k | d] = jnp.where(low, pltpu.roll(a, 128 - 16 * d, 1), b)
            for k in range(8):
                a_send[half * 8 + k, :, octet * 128:(octet + 1) * 128] = v[k].astype(BF16)

    pl.semaphore_wait(barrier, len(partners))

    loads["head"].wait()

    def near2(half, da, db):
        if half == 0:
            return shift(y, db) * 4 + shift(x, da)
        return shift(y, da) * 4 + shift(x, db)

    g_copies = {}

    def g_go(half, slot, rows, sem, to):
        lanes = pl.ds(half * 1024, 1024)
        where = gt.at[slot, pl.ds(rows[0], rows[1]), lanes]
        g_copies[half, sem] = go(copy(where, where, sg.at[half, sem], rg.at[half, sem], core, z, to))

    def g_wait(half, sem):
        wait(g_copies[half, sem])

    whole, upper, lower = (0, 32), (0, 16), (16, 16)

    a_copies = {}
    def start_a(offsets):
        for d in offsets:
            to = inplane(d)
            a_copies[d] = go(copy(a_send.at[to], a_recv.at[me], sa.at[d - 1], ra.at[d - 1], core, z, to))

    def start_g1():
        for half in range(2):
            g_go(half, me, whole, 0, near2(half, 1, 0))
            g_go(half, me, whole, 1, near2(half, -1, 0))

    def start_g2():
        for half in range(2):
            g_go(half, me, whole, 4, near2(half, 0, 1))
            g_go(half, me, whole, 5, near2(half, 0, -1))


    a_recv[me] = a_send[me]
    for step in START:
        {"A": lambda: start_a(AORD), "1": start_g1, "2": start_g2}[step]()

    def dot_across(piece):
        both = dot(across[...], piece, NT)
        return both[0:64] + both[64:128]

    for name in ("mom", "across", "pick", "project", "keep", "back", "spread"):
        loads[name].wait()
    wm_send[...] = jnp.zeros_like(wm_send)
    wg[...] = jnp.zeros_like(wg)
    for zz in range(LINE):
        piece = mom[:, zz * ZCOLS:(zz + 1) * ZCOLS]
        wm_send[zz, :, 0:RBLOCKS] = dot_across(piece)
    wm_copies = []

    def wm_start():
        for d in range(1, 4):
            to = shift(z, d)
            wm_copies.append(go(copy(wm_send.at[to], wm_recv.at[z], swm.at[d - 1], rwm.at[d - 1], core, to, me)))
        wm_recv[z] = wm_send[z]

    wm_start()

    z_copies = {}
    zu, zd, zo = shift(z, 1), shift(z, -1), shift(z, 2)
    every, first, second = (0, 320), (0, 160), (160, 160)

    def z_go(slot, dy, rows, sem, to):
        where = at.at[slot, shift(y, dy), pl.ds(rows[0], rows[1]), :]
        z_copies[dy, sem] = go(copy(where, where, sz.at[dy, sem], rz.at[dy, sem], core, to, me))

    def z_wait(dy, sem):
        wait(z_copies[dy, sem])

    def a_line(dy):
        for dx in range(4):
            d = (-dy % 4) * 4 + (-dx % 4)
            if d:
                wait(a_copies[d])
        line = shift(y, dy)
        tokens = a_recv[pl.ds(line * 4, 4)].reshape(128, 384)
        at[z, line] = dot(pick[...], tokens, NT).astype(BF16)
        z_go(z, dy, every, 0, zu)
        z_go(z, dy, every, 1, zd)

    def z_relay(dy):
        z_wait(dy, 0)
        z_go(zd, dy, first, 2, zu)
        z_wait(dy, 1)
        z_go(zu, dy, second, 3, zd)

    def g_relay(j, da):
        for half in range(2):
            g_wait(half, 4 + 4 * j)
            g_go(half, near2(half, da, -1), upper, 6 + 4 * j, near2(half, 0, 1))
            g_wait(half, 5 + 4 * j)
            g_go(half, near2(half, da, 1), lower, 7 + 4 * j, near2(half, 0, -1))

    def regroup_w(src, dst):
        for q in range(PLANE):
            for zz in range(LINE):
                dst[q, 4 * zz:4 * zz + 4, :] = src[zz, 4 * q:4 * q + 4, :]

    def regroup_v(src, dst):
        for q in range(PLANE):
            for zz in range(LINE):
                dst[zz, 4 * q:4 * q + 4, :] = src[q, 4 * zz:4 * zz + 4, :]

    def plane_start(src, dst, ssem, rsem):
        out = []
        for d in far_first:
            to = inplane(d)
            out.append(go(copy(src.at[to], dst.at[me], ssem.at[d - 1], rsem.at[d - 1], core, z, to)))
        dst[me] = src[me]
        return out

    def line_start(src, dst, ssem, rsem):
        out = {0: go(copy(src.at[z], dst.at[core, z], ssem.at[1, 0], rsem.at[1, 0], 1 - core, z, me))}
        for d in (2, 1, 3):
            to = shift(z, d)
            out[d] = go(copy(src.at[to], dst.at[core, z], ssem.at[0, d], rsem.at[0, d], core, to, me))
        dst[core, z] = src[z]
        return out

    def line_end(out, dst, ssem, rsem):
        forward = [out[0]]
        for d in (1, 3, 2):
            wait(out[d])
            where = dst.at[core, shift(z, -d)]
            forward.append(go(copy(where, where, ssem.at[1, d], rsem.at[1, d], 1 - core, z, me)))
        return forward

    def apply_project(w):
        high, low = parts(w)
        return dot(project[0], high, NN) + dot(project[0], low, NN) + dot(project[1], high, NN)

    pm_copies, qm_copies, vm_copies = [], [], []

    def momentum_step(which):
        if which == 1:
            for c in wm_copies:
                wait(c)
            regroup_w(wm_recv, pm_send)
            pm_copies.extend(plane_start(pm_send, pm_recv, spm, rpm))
        elif which == 2:
            for c in pm_copies:
                wait(c)
            qm_send[...] = apply_project(pm_recv[...].reshape(256, 128)).reshape(PLANE, 16, 128)
            qm_copies.extend(plane_start(qm_send, qm_recv, sqm, rqm))
        elif which == 3:
            for c in qm_copies:
                wait(c)
            regroup_v(qm_recv, vm)
            vm_copies.append(line_start(vm, vm_all, svm, rvm))
        else:
            for c in line_end(vm_copies[0], vm_all, svm, rvm):
                wait(c)
            for r in range(2):
                for zz in range(LINE):
                    for q in range(PLANE):
                        vm_rows[zz * 16 + q, 4 * r:4 * r + 4, :] = vm_all[r, zz, 4 * q:4 * q + 4, :]

    def near_chunks():
        for half in range(2):
            g_wait(half, 0)
            g_go(half, near2(half, -1, 0), upper, 2, near2(half, 1, 0))
            g_wait(half, 1)
            g_go(half, near2(half, 1, 0), lower, 3, near2(half, -1, 0))
        for half in range(2):
            for j, da in ((1, -1), (2, 1)):
                g_go(half, near2(half, da, 0), whole, 4 + 4 * j, near2(half, 0, 1))
                g_go(half, near2(half, da, 0), whole, 5 + 4 * j, near2(half, 0, -1))

    def far_chunk():
        for half in range(2):
            g_wait(half, 2)
            g_wait(half, 3)
            g_go(half, near2(half, 2, 0), whole, 16, near2(half, 0, 1))
            g_go(half, near2(half, 2, 0), whole, 17, near2(half, 0, -1))

    for step in ORDER:
        kind, which = step[0], step[1:]
        if kind == "a":
            a_line(int(which))
        elif kind == "z":
            z_relay(int(which))
        elif kind == "s":
            near_chunks()
        elif kind == "f":
            far_chunk()
        elif kind == "m":
            momentum_step(int(which))
        else:
            g_relay(int(which), (0, -1, 1, 2)[int(which)])

    for j in range(4):
        for half in range(2):
            g_wait(half, 6 + 4 * j)
            g_wait(half, 7 + 4 * j)
    for dy in (0, 1, 3, 2):
        z_wait(dy, 2)
        z_wait(dy, 3)

    grad_copies, pg_copies, qg_copies, vg_copies = [], [], [], []
    acc = None
    for zz in range(LINE):
        left = jnp.concatenate([at[zz, yy] for yy in range(4)], axis=1)
        term = dot(left, gt[:, :, zz * ZTOK:(zz + 1) * ZTOK].reshape(ZCOLS, ZTOK), NT)
        acc = term if acc is None else acc + term
    grad[...] = acc.reshape(LINE, RBLOCKS, ZCOLS)
    squares = jnp.zeros((8, 128), F32)
    for zz in range(LINE):
        piece = grad[zz]
        high, low = parts(piece)
        wg[zz, :, 0:RBLOCKS] = dot_across(high) + dot(across[0:64], low, NT)
        sq = piece * piece
        for lane in range(4):
            squares += jnp.sum(sq[:, lane * 128:(lane + 1) * 128].reshape(10, 8, 128), axis=0)
    regroup_w(wg, pg_send)
    for q in range(PLANE):
        pg_send[q, 16:24, :] = squares
    pg_copies = plane_start(pg_send, pg_recv, spg, rpg)
    for d in range(1, 4):
        to = shift(z, d)
        grad_copies.append(go(copy(grad.at[to], grad_row.at[z], sgr.at[d - 1], rgr.at[d - 1], core, to, me)))
    grad_row[z] = grad[z]
    for step in MSTEPS[0]:
        momentum_step(step)
    for c in pg_copies:
        wait(c)
    v_copies = {}
    high, low = parts(pg_recv[:, 0:16, :].reshape(256, 128))
    both = dot(keep[...], high, NN)
    coef[core, 0:32, :] = both[0:32] + both[32:64] + dot(keep[0:32], low, NN)
    plane_sq = jnp.sum(pg_recv[:, 16:24, :], axis=0)
    plane_sq = jnp.sum(jnp.sum(plane_sq, axis=0, keepdims=True), axis=1, keepdims=True)
    coef[core, 32:40, :] = jnp.broadcast_to(plane_sq, (8, 128))
    share = go(copy(coef.at[core], coef.at[core], sfg.at[0], rfg.at[0], 1 - core, z, me))
    wait(share)
    high, low = parts(jnp.concatenate([coef[0, 0:32], coef[1, 0:32]], axis=0))
    result = dot(back[...], jnp.concatenate([high, low, high], axis=0), NN)
    row = lax.broadcasted_iota(jnp.int32, (8, 128), 0)
    lane = lax.broadcasted_iota(jnp.int32, (8, 128), 1)
    sums = jnp.where(row < 4, coef[0, 32:40], coef[1, 32:40])
    vg[...] = result.reshape(64, 8, 128) + jnp.where(lane >= RBLOCKS, sums, F32(0.0))[None]
    for dz, d in sorted(((dz, d) for dz in range(4) for d in range(16)), key=lambda v: -hops(*v)):
        if dz or d:
            zz, ii = shift(z, dz), inplane(d)
            v_copies[dz, d] = go(copy(
                vg.at[zz * 16 + ii], vg_all.at[t], sqg.at[dz, d], rqg.at[dz, d], core, zz, ii))
    vg_all[t] = vg[t]
    for step in MSTEPS[1]:
        momentum_step(step)
    for c in v_copies.values():
        wait(c)

    factors = []
    for r in range(2):
        square = vg_all[0, 4 * r:4 * r + 1, 127:128]
        for zz in range(1, LINE):
            square = square + vg_all[zz * 16, 4 * r:4 * r + 1, 127:128]
        factors.append(jnp.minimum(F32(1.0), 1.0 / jnp.sqrt(square / (RBLOCKS * BLOCK * COLS) + 1e-06)))
    factor = jnp.where(core == 0, factors[0], factors[1])
    row = lax.broadcasted_iota(jnp.int32, (8, 128), 0)
    by_row = jnp.where(row < 4, factors[0], factors[1])
    total_v[...] = (F32(0.9) * vm_rows[...] + by_row[None] * vg_all[...]).reshape(512, 128)
    for c in grad_copies:
        wait(c)
    for g in range(8):
        cols = slice(g * 256, (g + 1) * 256)
        local = slice((g % 2) * 256, (g % 2) * 256 + 256)
        high, low = parts(total_v[g * 64:(g + 1) * 64, :])
        kept = dot(jnp.concatenate([high, low, high], axis=0), spread[core], TN)[0:RBLOCKS]
        full = F32(0.9) * mom[:, cols].astype(F32) + factor * grad_row[g // 2, :, local]
        new_out[:, cols] = (full - kept[:, 0:256]).astype(BF16)
        upd_out[:, cols] = kept[:, 256:512].astype(BF16)
    for c in sent:
        if id(c) not in arrived:
            c.wait_recv()
        c.wait_send()


def body(activations, head_grads, momentum):
    dma = pltpu.SemaphoreType.DMA
    consts = [jnp.asarray(c) for c in tables()]
    vmem = pl.BlockSpec(memory_space=pltpu.VMEM)
    hbm = pl.BlockSpec(memory_space=pltpu.HBM)
    scratch = [
        pltpu.VMEM((32, RBLOCKS * BLOCK), BF16),
        pltpu.VMEM((RBLOCKS, COLS), BF16),
    ] + [pltpu.VMEM(c.shape, BF16) for c in consts] + [
        pltpu.VMEM((640, 256), BF16),
        pltpu.VMEM((PLANE, 32, 384), BF16),
        pltpu.VMEM((PLANE, 32, 384), BF16),
        pltpu.VMEM((LINE, 4, 320, 128), BF16),
        pltpu.VMEM((PLANE, 32, TOKENS), BF16),
        pltpu.VMEM((LINE, RBLOCKS, ZCOLS), F32),
        pltpu.VMEM((LINE, RBLOCKS, ZCOLS), F32),
        pltpu.VMEM((LINE, 64, 128), F32),
        pltpu.VMEM((LINE, 64, 128), F32),
        pltpu.VMEM((PLANE, 16, 128), F32),
        pltpu.VMEM((PLANE, 16, 128), F32),
        pltpu.VMEM((PLANE, 16, 128), F32),
        pltpu.VMEM((PLANE, 16, 128), F32),
        pltpu.VMEM((LINE, 64, 128), F32),
        pltpu.VMEM((2, LINE, 64, 128), F32),
        pltpu.VMEM((LINE, 64, 128), F32),
        pltpu.VMEM((PLANE, 24, 128), F32),
        pltpu.VMEM((PLANE, 24, 128), F32),
        pltpu.VMEM((2, 40, 128), F32),
        pltpu.VMEM((64, 8, 128), F32),
        pltpu.VMEM((64, 8, 128), F32),
        pltpu.VMEM((64, 8, 128), F32),
        pltpu.VMEM((512, 128), F32),
        dma((10,)),
    ]
    for shape in ((15,), (4, 4), (2, 20), (3,), (3,), (15,), (15,), (2, 4), (15,), (4, 16), (1,)):
        scratch += [dma(shape), dma(shape)]
    new, upd = pl.pallas_call(
        kernel,
        out_shape=(
            pltpu.VMEM((RBLOCKS, COLS), BF16),
            pltpu.VMEM((RBLOCKS, COLS), BF16),
        ),
        in_specs=[hbm] * 10,
        out_specs=(vmem, vmem),
        scratch_shapes=scratch,
        compiler_params=pltpu.CompilerParams(
            collective_id=0, has_side_effects=True, vmem_limit_bytes=48 * 1024 * 1024
        ),
    )(*(pltpu.with_memory_space_constraint(v, pltpu.HBM)
        for v in (activations, head_grads.T, momentum.reshape(RBLOCKS, COLS), *consts)))

    def store(new_ref, upd_ref, new_hbm, upd_hbm, sems):
        copies = (
            pltpu.make_async_copy(new_ref, new_hbm, sems.at[0]),
            pltpu.make_async_copy(upd_ref, upd_hbm, sems.at[1]),
        )
        for c in copies:
            c.start()
        for c in copies:
            c.wait()

    new, upd = pl.pallas_call(
        store,
        out_shape=(
            jax.ShapeDtypeStruct((RBLOCKS, COLS), BF16),
            jax.ShapeDtypeStruct((RBLOCKS, COLS), BF16),
        ),
        in_specs=[vmem] * 2,
        out_specs=(hbm, hbm),
        scratch_shapes=[dma((2,))],
    )(*(pltpu.with_memory_space_constraint(v, pltpu.VMEM) for v in (new, upd)))
    return new[None, None], upd[None]


def solution(mesh):
    placed = (P(("dp", "tensor"), None), P("dp", "tensor"), P("dp", "tensor", None, None))
    return jax.shard_map(
        body,
        mesh=mesh,
        in_specs=placed,
        out_specs=(P("dp", "tensor", None, None), P("tensor", None, None)),
        check_vma=False,
    )
```

```python
import math

import jax
import jax.numpy as jnp
import ml_dtypes
import numpy as np
from jax import lax
from jax.experimental import pallas as pl
from jax.experimental.pallas import tpu as pltpu
from jax.sharding import PartitionSpec as P

BLOCK = 64
KEEP = 8
RBLOCKS = 80
COLS = 2048
TOKENS = 2048
LINE = 4
PLANE = 16
ZCOLS = COLS // LINE
ZTOK = TOKENS // LINE
OWN = 5
ROWS = 400
MESH = pl.DeviceIdType.MESH
F32 = jnp.float32
BF16 = jnp.bfloat16
NT = (((1,), (1,)), ((), ()))
TN = (((0,), (0,)), ((), ()))
NN = (((1,), (0,)), ((), ()))
ORDER = ("a0", "a1", "a3", "s", "a2", "m1", "g0", "z0", "f", "z1", "m2", "z3", "g1", "g2", "z2", "g3", "m3")
START = "A12"
MSTEPS = (4,)
AORD = (1, 3, 2, 4, 12, 5, 7, 13, 15, 6, 14, 8, 9, 11, 10)


def split(table):
    high = table.astype(np.float32).astype(ml_dtypes.bfloat16)
    low = (table - high.astype(np.float64)).astype(np.float32).astype(ml_dtypes.bfloat16)
    return high, low


def tables():
    k = np.arange(KEEP)[:, None]
    n = np.arange(BLOCK)[None, :]
    scale = np.where(k == 0, math.sqrt(1.0 / BLOCK), math.sqrt(2.0 / BLOCK))
    basis = scale * np.cos(math.pi * (2 * n + 1) * k / (2 * BLOCK))
    sort = np.zeros((256, 256))
    for a in range(4):
        for z in range(LINE):
            for i in range(PLANE):
                sort[a * 64 + z * 16 + i, i * 16 + z * 4 + a] = 1
    pick = np.zeros((ROWS, 640))
    for tile in range(RBLOCKS // 4):
        for z in range(LINE):
            for a in range(4):
                lane = tile * 16 + z * 4 + a
                pick[z * RBLOCKS + 4 * tile + a, lane] = 1
                if tile >= 16:
                    pick[z * RBLOCKS + 4 * tile + a, lane + 192] = 1
    for k in range(OWN * KEEP):
        pick[320 + k, 512 + k] = 1
        pick[360 + k, 576 + k] = 1
    squeeze = np.zeros((2, 384, 128))
    for odd in range(2):
        for part, table in enumerate(split(basis)):
            for j in range(OWN):
                top = (j + odd) * BLOCK
                squeeze[odd, top:top + BLOCK, part * 64 + j * KEEP:part * 64 + (j + 1) * KEEP] = table.T.astype(np.float64)
    across = np.kron(np.eye(8), basis)
    across_h, across_l = split(across)
    twice = np.stack([np.concatenate([v, v], axis=0) for v in (across_h, across_l)])
    expand = np.concatenate([across_h, across_h, across_l], axis=0)
    order = np.array([z * PLANE + i for i in range(PLANE) for z in range(LINE)])
    project = np.kron((basis.T @ basis)[np.ix_(order, order)], np.eye(4))
    back = np.zeros((BLOCK, 8, 48))
    for j in range(OWN):
        back[:, j, j * KEEP:(j + 1) * KEEP] = basis.T
    back_h, back_l = split(back.reshape(512, 48))
    back = np.concatenate([back_h, back_h, back_l], axis=1)
    spread = np.zeros((2, 2, 64, 2, 512))
    for r in range(2):
        spread[r, r, :, 0] = across
        spread[r, :, :, 1] = 0.5 * across
    spread_h, spread_l = split(spread.reshape(2, 128, 1024))
    spread = np.concatenate([spread_h, spread_h, spread_l], axis=1)
    return (
        sort.astype(ml_dtypes.bfloat16),
        pick.astype(ml_dtypes.bfloat16),
        squeeze.astype(ml_dtypes.bfloat16),
        twice,
        expand,
        np.stack(split(project)),
        back,
        spread,
    )


def dot(a, b, dims):
    return lax.dot_general(a, b, dims, preferred_element_type=F32)


def parts(x):
    high = x.astype(BF16)
    return high, (x - high.astype(F32)).astype(BF16)


def kernel(
    act_hbm, head_hbm, mom_hbm, sort_hbm, pick_hbm, squeeze_hbm, twice_hbm, expand_hbm, project_hbm, back_hbm, spread_hbm,
    new_out, upd_out,
    act, mom, sort, pick, squeeze, twice, expand, project, back, spread, stack, windows,
    a_send, a_recv, tokens, at, gt, grad, grad_row,
    wm_send, wm_recv, pm_send, pm_recv, qm_send, qm_recv, vm, vm_all,
    coef, vg, vg_all, packed, base_new, base_upd,
    load, sa, ra, sz, rz, sg, rg, sgr, rgr, swm, rwm,
    spm, rpm, sqm, rqm, svm, rvm, sqg, rqg, sfg, rfg,
):
    core = lax.axis_index("dp")
    t = lax.axis_index("tensor")
    z, me = lax.div(t, 16), lax.rem(t, 16)
    y, x = lax.div(me, 4), lax.rem(me, 4)

    def shift(v, by):
        return lax.rem(v + by % 4, 4)

    def inplane(d):
        return shift(y, d // 4) * 4 + shift(x, d % 4)

    def hops(dz, d):
        return sum(min(v, 4 - v) for v in (dz, d // 4, d % 4))

    far_first = sorted(range(1, 16), key=lambda d: -hops(0, d))

    def copy(src, dst, ssem, rsem, c, zz, ii):
        return pltpu.make_async_remote_copy(
            src_ref=src, dst_ref=dst, send_sem=ssem, recv_sem=rsem,
            device_id=(c, zz * 16 + ii), device_id_type=MESH,
        )

    sent = []
    arrived = set()

    def go(c):
        c.start()
        sent.append(c)
        return c

    def wait(c):
        c.wait_recv()
        arrived.add(id(c))

    barrier = pltpu.get_barrier_semaphore()
    partners = [(core, z, inplane(d)) for d in far_first]
    partners += [(core, shift(z, d), me) for d in (2, 1, 3)] + [(1 - core, z, me)]
    for c, zz, ii in partners:
        pl.semaphore_signal(barrier, inc=1, device_id=(c, zz * 16 + ii), device_id_type=MESH)

    loads = {}
    for k, (name, src, dst) in enumerate((
        ("act", act_hbm, act), ("sort", sort_hbm, sort), ("squeeze", squeeze_hbm, squeeze), ("head", head_hbm, gt.at[me]),
        ("mom", mom_hbm, mom), ("pick", pick_hbm, pick), ("twice", twice_hbm, twice), ("expand", expand_hbm, expand),
        ("project", project_hbm, project), ("back", back_hbm, back), ("spread", spread_hbm.at[core], spread),
    )):
        loads[name] = pltpu.make_async_copy(src, dst, load.at[k])
        loads[name].start()

    loads["act"].wait()
    loads["sort"].wait()
    for tile in range(20):
        stack[tile * 32:(tile + 1) * 32, :] = act[:, tile * 256:(tile + 1) * 256]
    sorted_cols = dot(stack[...], sort[...], NN)
    group = lax.broadcasted_iota(jnp.int32, (32, 128), 1) // 16
    zero = jnp.zeros((32, 128), F32)
    for half in range(2):
        for octet in range(3):
            v = []
            for tile in range(octet * 8, octet * 8 + 8):
                if tile < 20:
                    v.append(sorted_cols[tile * 32:(tile + 1) * 32, half * 128:(half + 1) * 128])
                else:
                    v.append(zero)
            for d in (1, 2, 4):
                low = (group // d) % 2 == 0
                for k in range(8):
                    if k & d == 0:
                        a, b = v[k], v[k | d]
                        v[k] = jnp.where(low, a, pltpu.roll(b, 16 * d, 1))
                        v[k | d] = jnp.where(low, pltpu.roll(a, 128 - 16 * d, 1), b)
            for k in range(8):
                upper_rows, lower_rows = v[k][0:16], v[k][16:32]
                if octet < 2:
                    a_send[half * 8 + k, :, octet * 128:octet * 128 + 128] = upper_rows.astype(BF16)
                    a_send[half * 8 + k, :, octet * 128 + 256:octet * 128 + 384] = lower_rows.astype(BF16)
                else:
                    folded = jnp.where(group[0:16] < 4, upper_rows, pltpu.roll(lower_rows, 64, 1))
                    a_send[half * 8 + k, :, 512:640] = folded.astype(BF16)

    loads["squeeze"].wait()
    first_half = lax.broadcasted_iota(jnp.int32, (256, 128), 1) < 64
    for odd in range(2):
        for m in range(8):
            windows[odd, m * 32:(m + 1) * 32, :] = act[:, m * 640 + odd * 256:m * 640 + odd * 256 + 384]
        both = dot(windows[odd], squeeze[odd], NN)
        both = both + pltpu.roll(both, 64, 1)
        high = both.astype(BF16).astype(F32)
        both = jnp.where(first_half, high, both - high).astype(BF16)
        for m in range(8):
            a_send[2 * m + odd, :, 640:768] = both[m * 32:m * 32 + 16]
            a_send[2 * m + odd, :, 768:896] = both[m * 32 + 16:m * 32 + 32]

    for name in ("mom", "twice"):
        loads[name].wait()
    wm_send[...] = jnp.zeros_like(wm_send)
    coef[core] = jnp.zeros((56, 128), F32)
    for zz in range(LINE):
        piece = mom[:, zz * ZCOLS:(zz + 1) * ZCOLS]
        wm_send[zz, :, 0:RBLOCKS] = dot(twice[0, 0:64], piece, NT) + dot(twice[1, 0:64], piece, NT)
    pl.semaphore_wait(barrier, len(partners))

    wm_copies = []

    def wm_start():
        for d in range(1, 4):
            to = shift(z, d)
            wm_copies.append(go(copy(wm_send.at[to], wm_recv.at[z], swm.at[d - 1], rwm.at[d - 1], core, to, me)))
        wm_recv[z] = wm_send[z]

    wm_start()


    loads["head"].wait()

    def near2(half, da, db):
        if half == 0:
            return shift(y, db) * 4 + shift(x, da)
        return shift(y, da) * 4 + shift(x, db)

    g_copies = {}

    def g_go(half, slot, rows, sem, to):
        lanes = pl.ds(half * 1024, 1024)
        where = gt.at[slot, pl.ds(rows[0], rows[1]), lanes]
        g_copies[half, sem] = go(copy(where, where, sg.at[half, sem], rg.at[half, sem], core, z, to))

    def g_wait(half, sem):
        wait(g_copies[half, sem])

    whole, upper, lower = (0, 32), (0, 16), (16, 16)

    a_copies = {}
    def start_a(offsets):
        for d in offsets:
            to = inplane(d)
            a_copies[d] = go(copy(a_send.at[to], a_recv.at[me], sa.at[d - 1], ra.at[d - 1], core, z, to))

    def start_g1():
        for half in range(2):
            g_go(half, me, whole, 0, near2(half, 1, 0))
            g_go(half, me, whole, 1, near2(half, -1, 0))

    def start_g2():
        for half in range(2):
            g_go(half, me, whole, 4, near2(half, 0, 1))
            g_go(half, me, whole, 5, near2(half, 0, -1))


    a_recv[me] = a_send[me]
    tokens[...] = jnp.zeros_like(tokens)
    for step in START:
        {"A": lambda: start_a(AORD), "1": start_g1, "2": start_g2}[step]()

    for name in ("pick", "expand", "project", "back", "spread"):
        loads[name].wait()

    z_copies = {}
    zu, zd, zo = shift(z, 1), shift(z, -1), shift(z, 2)
    every, first, second = (0, 400), (0, 208), (208, 192)

    def z_go(slot, dy, rows, sem, to):
        where = at.at[slot, shift(y, dy), pl.ds(rows[0], rows[1]), :]
        z_copies[dy, sem] = go(copy(where, where, sz.at[dy, sem], rz.at[dy, sem], core, to, me))

    def z_wait(dy, sem):
        wait(z_copies[dy, sem])

    def a_line(dy):
        for dx in range(4):
            d = (-dy % 4) * 4 + (-dx % 4)
            if d:
                wait(a_copies[d])
        line = shift(y, dy)
        for src in range(4):
            here = a_recv.at[line * 4 + src]
            top, low = slice(src * 32, src * 32 + 16), slice(src * 32 + 16, src * 32 + 32)
            tokens[top, 0:256] = here[:, 0:256]
            tokens[top, 256:384] = here[:, 512:640]
            tokens[low, 0:256] = here[:, 256:512]
            tokens[low, 384:512] = here[:, 512:640]
            tokens[top, 512:640] = here[:, 640:768]
            tokens[low, 512:640] = here[:, 768:896]
        at[z, line] = dot(pick[...], tokens[...], NT).astype(BF16)
        z_go(z, dy, every, 0, zu)
        z_go(z, dy, every, 1, zd)

    def z_relay(dy):
        z_wait(dy, 0)
        z_go(zd, dy, first, 2, zu)
        z_wait(dy, 1)
        z_go(zu, dy, second, 3, zd)

    def g_relay(j, da):
        for half in range(2):
            g_wait(half, 4 + 4 * j)
            g_go(half, near2(half, da, -1), upper, 6 + 4 * j, near2(half, 0, 1))
            g_wait(half, 5 + 4 * j)
            g_go(half, near2(half, da, 1), lower, 7 + 4 * j, near2(half, 0, -1))

    def regroup_w(src, dst):
        for q in range(PLANE):
            for zz in range(LINE):
                dst[q, 4 * zz:4 * zz + 4, :] = src[zz, 4 * q:4 * q + 4, :]

    def regroup_v(src, dst):
        for q in range(PLANE):
            for zz in range(LINE):
                dst[zz, 4 * q:4 * q + 4, :] = src[q, 4 * zz:4 * zz + 4, :]

    def plane_start(src, dst, ssem, rsem):
        out = []
        for d in far_first:
            to = inplane(d)
            out.append(go(copy(src.at[to], dst.at[me], ssem.at[d - 1], rsem.at[d - 1], core, z, to)))
        dst[me] = src[me]
        return out

    def line_start(src, dst, ssem, rsem):
        out = {0: go(copy(src.at[z], dst.at[core, z], ssem.at[1, 0], rsem.at[1, 0], 1 - core, z, me))}
        for d in (2, 1, 3):
            to = shift(z, d)
            out[d] = go(copy(src.at[to], dst.at[core, z], ssem.at[0, d], rsem.at[0, d], core, to, me))
        dst[core, z] = src[z]
        return out

    def line_end(out, dst, ssem, rsem):
        forward = [out[0]]
        for d in (1, 3, 2):
            wait(out[d])
            where = dst.at[core, shift(z, -d)]
            forward.append(go(copy(where, where, ssem.at[1, d], rsem.at[1, d], 1 - core, z, me)))
        return forward

    def apply_project(w):
        high, low = parts(w)
        return dot(project[0], high, NN) + dot(project[0], low, NN) + dot(project[1], high, NN)

    pm_copies, qm_copies, vm_copies = [], [], []

    def momentum_step(which):
        if which == 1:
            for c in wm_copies:
                wait(c)
            regroup_w(wm_recv, pm_send)
            pm_copies.extend(plane_start(pm_send, pm_recv, spm, rpm))
        elif which == 2:
            for c in pm_copies:
                wait(c)
            qm_send[...] = apply_project(pm_recv[...].reshape(256, 128)).reshape(PLANE, 16, 128)
            qm_copies.extend(plane_start(qm_send, qm_recv, sqm, rqm))
        elif which == 3:
            for c in qm_copies:
                wait(c)
            regroup_v(qm_recv, vm)
            vm_copies.append(line_start(vm, vm_all, svm, rvm))
        else:
            for c in line_end(vm_copies[0], vm_all, svm, rvm):
                wait(c)
            for zz in range(LINE):
                cols = slice(zz * ZCOLS, (zz + 1) * ZCOLS)
                pair = []
                for r in range(2):
                    high, low = parts(vm_all[r, zz])
                    pair.append(dot(jnp.concatenate([high, low, high], axis=0), expand[...], TN)[0:RBLOCKS])
                base_upd[:, cols] = F32(0.45) * (pair[0] + pair[1])
                own = jnp.where(core == 0, pair[0], pair[1])
                base_new[:, cols] = F32(0.9) * (mom[:, cols].astype(F32) - own)

    def near_chunks():
        for half in range(2):
            g_wait(half, 0)
            g_go(half, near2(half, -1, 0), upper, 2, near2(half, 1, 0))
            g_wait(half, 1)
            g_go(half, near2(half, 1, 0), lower, 3, near2(half, -1, 0))
        for half in range(2):
            for j, da in ((1, -1), (2, 1)):
                g_go(half, near2(half, da, 0), whole, 4 + 4 * j, near2(half, 0, 1))
                g_go(half, near2(half, da, 0), whole, 5 + 4 * j, near2(half, 0, -1))

    def far_chunk():
        for half in range(2):
            g_wait(half, 2)
            g_wait(half, 3)
            g_go(half, near2(half, 2, 0), whole, 16, near2(half, 0, 1))
            g_go(half, near2(half, 2, 0), whole, 17, near2(half, 0, -1))

    for step in ORDER:
        kind, which = step[0], step[1:]
        if kind == "a":
            a_line(int(which))
        elif kind == "z":
            z_relay(int(which))
        elif kind == "s":
            near_chunks()
        elif kind == "f":
            far_chunk()
        elif kind == "m":
            momentum_step(int(which))
        else:
            g_relay(int(which), (0, -1, 1, 2)[int(which)])

    for j in range(4):
        for half in range(2):
            g_wait(half, 6 + 4 * j)
            g_wait(half, 7 + 4 * j)
    grad_copies = []

    def term(zz):
        left = jnp.concatenate([at[zz, yy] for yy in range(4)], axis=1)
        right = gt[:, :, pl.ds(pl.multiple_of(zz * ZTOK, ZTOK), ZTOK)]
        return dot(left, right.reshape(ZCOLS, ZTOK), NT)

    acc = term(z) + term(zd) + term(zu)
    for dy in (0, 1, 3, 2):
        z_wait(dy, 2)
        z_wait(dy, 3)
    acc = acc + term(zo)
    rows = acc[0:320]
    grad[...] = rows.reshape(LINE, RBLOCKS, ZCOLS)
    square = jnp.sum(jnp.sum(rows * rows, axis=0, keepdims=True), axis=1, keepdims=True)
    for d in range(1, 4):
        to = shift(z, d)
        grad_copies.append(go(copy(grad.at[to], grad_row.at[z], sgr.at[d - 1], rgr.at[d - 1], core, to, me)))
    grad_row[z] = grad[z]
    mine = lax.broadcasted_iota(jnp.int32, (40, 128), 1) // 64 == core
    high, low = parts(acc[320:360] + acc[360:400])
    own = dot(high, twice[0], NT) + dot(low, twice[0], NT) + dot(high, twice[1], NT)
    coef[core, 0:40, :] = jnp.where(mine, own, F32(0.0))
    coef[core, 48:56, :] = jnp.where(mine[0:8], jnp.broadcast_to(square, (8, 128)), F32(0.0))
    share = go(copy(coef.at[core], coef.at[core], sfg.at[0], rfg.at[0], 1 - core, z, me))
    v_copies = {}
    wait(share)
    high, low = parts(coef[0, 0:48] + coef[1, 0:48])
    result = dot(back[...], jnp.concatenate([high, low, high], axis=0), NN)
    sums = coef[0, 48:56] + coef[1, 48:56]
    row = lax.broadcasted_iota(jnp.int32, (8, 128), 0)
    vg[...] = result.reshape(64, 8, 128) + jnp.where(row == 5, sums, F32(0.0))[None]
    for dz, d in sorted(((dz, d) for dz in range(4) for d in range(16)), key=lambda v: -hops(*v)):
        if dz or d:
            zz, ii = shift(z, dz), inplane(d)
            v_copies[dz, d] = go(copy(
                vg.at[zz * 16 + ii], vg_all.at[t], sqg.at[dz, d], rqg.at[dz, d], core, zz, ii))
    vg_all[t] = vg[t]
    for step in MSTEPS:
        momentum_step(step)
    for c in v_copies.values():
        wait(c)

    square = jnp.sum(vg_all[:, 5:6, :], axis=0)
    factors = jnp.minimum(F32(1.0), 1.0 / jnp.sqrt(square / (RBLOCKS * BLOCK * COLS) + 1e-06))
    factor = jnp.where(core == 0, factors[:, 0:1], factors[:, 127:128])
    for zz in range(LINE):
        for i in range(PLANE):
            packed[zz * RBLOCKS + OWN * i:zz * RBLOCKS + OWN * (i + 1), :] = vg_all[zz * 16 + i, 0:OWN, :]
    high, low = parts(packed[...] * factors)
    kept = dot(jnp.concatenate([high, low, high], axis=1), spread[...], NN)
    for c in grad_copies:
        wait(c)
    for zz in range(LINE):
        cols = slice(zz * ZCOLS, (zz + 1) * ZCOLS)
        rows = slice(zz * RBLOCKS, (zz + 1) * RBLOCKS)
        new_out[:, cols] = (base_new[:, cols] + (factor * grad_row[zz] - kept[rows, 0:512])).astype(BF16)
        upd_out[:, cols] = (base_upd[:, cols] + kept[rows, 512:1024]).astype(BF16)
    for c in sent:
        if id(c) not in arrived:
            c.wait_recv()
        c.wait_send()


def body(activations, head_grads, momentum):
    dma = pltpu.SemaphoreType.DMA
    consts = [jnp.asarray(c) for c in tables()]
    vmem = pl.BlockSpec(memory_space=pltpu.VMEM)
    hbm = pl.BlockSpec(memory_space=pltpu.HBM)
    scratch = [
        pltpu.VMEM((32, RBLOCKS * BLOCK), BF16),
        pltpu.VMEM((RBLOCKS, COLS), BF16),
    ] + [pltpu.VMEM(c.shape, BF16) for c in consts[:-1]] + [pltpu.VMEM(consts[-1].shape[1:], BF16)] + [
        pltpu.VMEM((640, 256), BF16),
        pltpu.VMEM((2, 256, 384), BF16),
        pltpu.VMEM((PLANE, 16, 896), BF16),
        pltpu.VMEM((PLANE, 16, 896), BF16),
        pltpu.VMEM((128, 640), BF16),
        pltpu.VMEM((LINE, 4, ROWS, 128), BF16),
        pltpu.VMEM((PLANE, 32, TOKENS), BF16),
        pltpu.VMEM((LINE, RBLOCKS, ZCOLS), F32),
        pltpu.VMEM((LINE, RBLOCKS, ZCOLS), F32),
        pltpu.VMEM((LINE, 64, 128), F32),
        pltpu.VMEM((LINE, 64, 128), F32),
        pltpu.VMEM((PLANE, 16, 128), F32),
        pltpu.VMEM((PLANE, 16, 128), F32),
        pltpu.VMEM((PLANE, 16, 128), F32),
        pltpu.VMEM((PLANE, 16, 128), F32),
        pltpu.VMEM((LINE, 64, 128), F32),
        pltpu.VMEM((2, LINE, 64, 128), F32),
        pltpu.VMEM((2, 56, 128), F32),
        pltpu.VMEM((64, 8, 128), F32),
        pltpu.VMEM((64, 8, 128), F32),
        pltpu.VMEM((LINE * RBLOCKS, 128), F32),
        pltpu.VMEM((RBLOCKS, COLS), F32),
        pltpu.VMEM((RBLOCKS, COLS), F32),
        dma((11,)),
    ]
    for shape in ((15,), (4, 4), (2, 20), (3,), (3,), (15,), (15,), (2, 4), (4, 16), (1,)):
        scratch += [dma(shape), dma(shape)]
    new, upd = pl.pallas_call(
        kernel,
        out_shape=(
            pltpu.VMEM((RBLOCKS, COLS), BF16),
            pltpu.VMEM((RBLOCKS, COLS), BF16),
        ),
        in_specs=[hbm] * 11,
        out_specs=(vmem, vmem),
        scratch_shapes=scratch,
        compiler_params=pltpu.CompilerParams(
            collective_id=0, has_side_effects=True, vmem_limit_bytes=48 * 1024 * 1024
        ),
    )(*(pltpu.with_memory_space_constraint(v, pltpu.HBM)
        for v in (activations, head_grads.T, momentum.reshape(RBLOCKS, COLS), *consts)))

    def store(new_ref, upd_ref, new_hbm, upd_hbm, sems):
        copies = (
            pltpu.make_async_copy(new_ref, new_hbm, sems.at[0]),
            pltpu.make_async_copy(upd_ref, upd_hbm, sems.at[1]),
        )
        for c in copies:
            c.start()
        for c in copies:
            c.wait()

    new, upd = pl.pallas_call(
        store,
        out_shape=(
            jax.ShapeDtypeStruct((RBLOCKS, COLS), BF16),
            jax.ShapeDtypeStruct((RBLOCKS, COLS), BF16),
        ),
        in_specs=[vmem] * 2,
        out_specs=(hbm, hbm),
        scratch_shapes=[dma((2,))],
    )(*(pltpu.with_memory_space_constraint(v, pltpu.VMEM) for v in (new, upd)))
    return new[None, None], upd[None]


def solution(mesh):
    placed = (P(("dp", "tensor"), None), P("dp", "tensor"), P("dp", "tensor", None, None))
    return jax.shard_map(
        body,
        mesh=mesh,
        in_specs=placed,
        out_specs=(P("dp", "tensor", None, None), P("tensor", None, None)),
        check_vma=False,
    )
```

```python
import math

import jax
import jax.numpy as jnp
import ml_dtypes
import numpy as np
from jax import lax
from jax.experimental import pallas as pl
from jax.experimental.pallas import tpu as pltpu
from jax.sharding import PartitionSpec as P

BLOCK = 64
KEEP = 8
RBLOCKS = 80
COLS = 2048
TOKENS = 2048
LINE = 4
PLANE = 16
ZCOLS = COLS // LINE
ZTOK = TOKENS // LINE
OWN = 5
SHARE = 1024
ROWS = 400
MESH = pl.DeviceIdType.MESH
F32 = jnp.float32
BF16 = jnp.bfloat16
NT = (((1,), (1,)), ((), ()))
TN = (((0,), (0,)), ((), ()))
NN = (((1,), (0,)), ((), ()))
ORDER = ("a0", "s", "a1", "a3", "a2", "m1", "f", "g0", "z0", "g1", "g2", "z1", "m2", "g3", "z3", "z2", "m3")
START = "1A2"
MSTEPS = (4,)
AORD = (1, 3, 2, 4, 12, 5, 7, 13, 15, 6, 14, 8, 9, 11, 10)


def split(table):
    high = table.astype(np.float32).astype(ml_dtypes.bfloat16)
    low = (table - high.astype(np.float64)).astype(np.float32).astype(ml_dtypes.bfloat16)
    return high, low


def device(core, line, place):
    return line * 16 + place + core * (place // 4 * 16 + line * 4 + place % 4 - line * 16 - place)


def tables():
    k = np.arange(KEEP)[:, None]
    n = np.arange(BLOCK)[None, :]
    scale = np.where(k == 0, math.sqrt(1.0 / BLOCK), math.sqrt(2.0 / BLOCK))
    basis = scale * np.cos(math.pi * (2 * n + 1) * k / (2 * BLOCK))
    sort = np.zeros((2, 256, 256))
    for a in range(4):
        for z in range(LINE):
            for i in range(PLANE):
                for core in range(2):
                    sort[core, a * 64 + device(core, z, i), i * 16 + z * 4 + a] = 1
    pick = np.zeros((ROWS, 640))
    for tile in range(RBLOCKS // 4):
        for z in range(LINE):
            for a in range(4):
                lane = tile * 16 + z * 4 + a
                pick[z * RBLOCKS + 4 * tile + a, lane] = 1
                if tile >= 16:
                    pick[z * RBLOCKS + 4 * tile + a, lane + 192] = 1
    for k in range(OWN * KEEP):
        pick[320 + k, 512 + k] = 1
        pick[360 + k, 576 + k] = 1
    squeeze = np.zeros((2, 384, 128))
    for odd in range(2):
        for part, table in enumerate(split(basis)):
            for j in range(OWN):
                top = (j + odd) * BLOCK
                squeeze[odd, top:top + BLOCK, part * 64 + j * KEEP:part * 64 + (j + 1) * KEEP] = table.T.astype(np.float64)
    across = np.kron(np.eye(8), basis)
    across_h, across_l = split(across)
    twice = np.stack([np.concatenate([v, v], axis=0) for v in (across_h, across_l)])
    expand = np.concatenate([across_h, across_h, across_l], axis=0)
    project = []
    for core in range(2):
        order = np.array([device(core, z, i) for i in range(PLANE) for z in range(LINE)])
        project.append(np.stack(split(np.kron((basis.T @ basis)[np.ix_(order, order)], np.eye(4)))))
    back = np.zeros((BLOCK, 8, 48))
    for j in range(OWN):
        back[:, j, j * KEEP:(j + 1) * KEEP] = basis.T
    back_h, back_l = split(back.reshape(512, 48))
    back = np.concatenate([back_h, back_h, back_l], axis=1)
    spread = np.zeros((2, 2, 64, 512))
    for r in range(2):
        spread[r, r] = across
    spread_h, spread_l = split(spread.reshape(2, 128, 512))
    spread = np.concatenate([spread_h, spread_h, spread_l], axis=1)
    return (
        sort.astype(ml_dtypes.bfloat16),
        pick.astype(ml_dtypes.bfloat16),
        squeeze.astype(ml_dtypes.bfloat16),
        twice,
        expand,
        np.stack(project),
        back,
        spread,
    )


def dot(a, b, dims):
    return lax.dot_general(a, b, dims, preferred_element_type=F32)


def parts(x):
    high = x.astype(BF16)
    return high, (x - high.astype(F32)).astype(BF16)


def kernel(
    act_hbm, head_hbm, mom_hbm, sort_hbm, pick_hbm, squeeze_hbm, twice_hbm, expand_hbm, project_hbm, back_hbm, spread_hbm,
    new_out, upd_out,
    act, head, mom, sort, pick, squeeze, twice, expand, project, back, spread, stack, windows,
    a_send, a_recv, tokens, at, gt, grad, grad_row,
    wm_send, wm_recv, pm_send, pm_recv, qm_send, qm_recv, vm, vm_all,
    coef, vg, vg_all, packed, kept, base_new, base_upd,
    load, sa, ra, sz, rz, sg, rg, sgr, rgr, swm, rwm,
    spm, rpm, sqm, rqm, svm, rvm, sqg, rqg, sfg, rfg,
):
    core = lax.axis_index("dp")
    t = lax.axis_index("tensor")
    zp, yp, x = lax.div(t, 16), lax.rem(lax.div(t, 4), 4), lax.rem(t, 4)
    z, y = zp + core * (yp - zp), yp + core * (zp - yp)
    me = y * 4 + x

    def around(v):
        return [v] + [lax.rem(v + by, 4) for by in range(1, 4)]

    zs, ys, xs, zps, yps = around(z), around(y), around(x), around(zp), around(yp)
    z_steps = [v * (16 - 12 * core) for v in zs]
    y_steps = [v * (4 + 12 * core) for v in ys]
    y_slots = [v * 4 for v in ys]
    zp_steps, yp_steps = [v * 16 for v in zps], [v * 4 for v in yps]

    def inplane(d):
        return y_slots[d // 4] + xs[d % 4]

    def place(dz, d):
        return z_steps[dz % 4] + y_steps[d // 4] + xs[d % 4]

    def hops(dz, d):
        return sum(min(v, 4 - v) for v in (dz, d // 4, d % 4))

    far_first = sorted(range(1, 16), key=lambda d: -hops(0, d))

    def copy_to(src, dst, ssem, rsem, where):
        return pltpu.make_async_remote_copy(
            src_ref=src, dst_ref=dst, send_sem=ssem, recv_sem=rsem, device_id=where, device_id_type=MESH,
        )

    def copy(src, dst, ssem, rsem, dz, d):
        return copy_to(src, dst, ssem, rsem, (core, place(dz, d)))

    def copy_across(src, dst, ssem, rsem):
        return copy_to(src, dst, ssem, rsem, (1 - core, t))

    sent = []
    arrived = set()

    def go(c):
        c.start()
        sent.append(c)
        return c

    def wait(c):
        c.wait_recv()
        arrived.add(id(c))

    barrier = pltpu.get_barrier_semaphore()
    partners = [(core, place(0, d)) for d in far_first]
    partners += [(core, place(d, 0)) for d in (2, 1, 3)] + [(1 - core, t)]
    for where in partners:
        pl.semaphore_signal(barrier, inc=1, device_id=where, device_id_type=MESH)

    loads = {}
    for k, (name, src, dst) in enumerate((
        ("act", act_hbm, act), ("sort", sort_hbm.at[core], sort), ("squeeze", squeeze_hbm, squeeze), ("head", head_hbm, head),
        ("mom", mom_hbm, mom), ("pick", pick_hbm, pick), ("twice", twice_hbm, twice), ("expand", expand_hbm, expand),
        ("project", project_hbm.at[core], project), ("back", back_hbm, back), ("spread", spread_hbm, spread),
    )):
        loads[name] = pltpu.make_async_copy(src, dst, load.at[k])
        loads[name].start()
    loads["act"].wait()
    loads["sort"].wait()
    for tile in range(20):
        stack[tile * 32:(tile + 1) * 32, :] = act[:, tile * 256:(tile + 1) * 256]
    sorted_cols = dot(stack[...], sort[...], NN)
    group = lax.broadcasted_iota(jnp.int32, (32, 128), 1) // 16
    zero = jnp.zeros((32, 128), F32)
    for half in range(2):
        for octet in range(3):
            v = []
            for tile in range(octet * 8, octet * 8 + 8):
                if tile < 20:
                    v.append(sorted_cols[tile * 32:(tile + 1) * 32, half * 128:(half + 1) * 128])
                else:
                    v.append(zero)
            for d in (1, 2, 4):
                low = (group // d) % 2 == 0
                for k in range(8):
                    if k & d == 0:
                        a, b = v[k], v[k | d]
                        v[k] = jnp.where(low, a, pltpu.roll(b, 16 * d, 1))
                        v[k | d] = jnp.where(low, pltpu.roll(a, 128 - 16 * d, 1), b)
            for k in range(8):
                upper_rows, lower_rows = v[k][0:16], v[k][16:32]
                if octet < 2:
                    a_send[half * 8 + k, :, octet * 128:octet * 128 + 128] = upper_rows.astype(BF16)
                    a_send[half * 8 + k, :, octet * 128 + 256:octet * 128 + 384] = lower_rows.astype(BF16)
                else:
                    folded = jnp.where(group[0:16] < 4, upper_rows, pltpu.roll(lower_rows, 64, 1))
                    a_send[half * 8 + k, :, 512:640] = folded.astype(BF16)

    loads["squeeze"].wait()
    first_half = lax.broadcasted_iota(jnp.int32, (256, 128), 1) < 64
    for odd in range(2):
        for m in range(8):
            windows[odd, m * 32:(m + 1) * 32, :] = act[:, m * 640 + odd * 256:m * 640 + odd * 256 + 384]
        both = dot(windows[odd], squeeze[odd], NN)
        both = both + pltpu.roll(both, 64, 1)
        high = both.astype(BF16).astype(F32)
        both = jnp.where(first_half, high, both - high).astype(BF16)
        for m in range(8):
            a_send[2 * m + odd, :, 640:768] = both[m * 32:m * 32 + 16]
            a_send[2 * m + odd, :, 768:896] = both[m * 32 + 16:m * 32 + 32]

    def chunk(line, q):
        return pl.ds(pl.multiple_of((line * 4 + q + core * (q * 4 + line - line * 4 - q)) * 128, 128), 128)

    for name in ("mom", "twice"):
        loads[name].wait()
    wm_send[...] = jnp.zeros_like(wm_send)
    coef[core] = jnp.zeros((56, 128), F32)
    for zz in range(LINE):
        piece = jnp.concatenate([mom[:, chunk(zz, q)] for q in range(4)], axis=1)
        wm_send[zz, :, 0:RBLOCKS] = dot(twice[0, 0:64], piece, NT) + dot(twice[1, 0:64], piece, NT)
    loads["head"].wait()
    for tile in range(16):
        line, row = tile // 4, tile % 4
        lanes = pl.ds(pl.multiple_of((tile + core * (row * 4 + line - tile)) * 128, 128), 128)
        gt[me, :, tile * 128:(tile + 1) * 128] = head[:, lanes]

    pl.semaphore_wait(barrier, len(partners))

    wm_copies = []

    def wm_start():
        for d in range(1, 4):
            to = zs[d]
            wm_copies.append(go(copy(wm_send.at[to], wm_recv.at[z], swm.at[d - 1], rwm.at[d - 1], d, 0)))
        wm_recv[z] = wm_send[z]

    wm_start()


    def offset(half, da, db):
        return (db % 4 * 4 + da % 4) if half == 0 else (da % 4 * 4 + db % 4)

    def near2(half, da, db):
        return inplane(offset(half, da, db))

    g_copies = {}

    def g_go(half, slot, rows, sem, to):
        lanes = pl.ds(0, SHARE) if half == 0 else pl.ds(SHARE, TOKENS - SHARE)
        where = gt.at[slot, pl.ds(rows[0], rows[1]), lanes]
        g_copies[half, sem] = go(copy(where, where, sg.at[half, sem], rg.at[half, sem], 0, to))

    def g_wait(half, sem):
        wait(g_copies[half, sem])

    whole, upper, lower = (0, 32), (0, 16), (16, 16)

    a_copies = {}
    def start_a(offsets):
        for d in offsets:
            to = inplane(d)
            a_copies[d] = go(copy(a_send.at[to], a_recv.at[me], sa.at[d - 1], ra.at[d - 1], 0, d))

    def start_g1():
        for half in range(2):
            g_go(half, me, whole, 0, offset(half, 1, 0))
            g_go(half, me, whole, 1, offset(half, -1, 0))

    def start_g2():
        for half in range(2):
            g_go(half, me, whole, 4, offset(half, 0, 1))
            g_go(half, me, whole, 5, offset(half, 0, -1))


    a_recv[me] = a_send[me]
    tokens[...] = jnp.zeros_like(tokens)
    for step in START:
        {"A": lambda: start_a(AORD), "1": start_g1, "2": start_g2}[step]()

    for name in ("pick", "expand", "project", "back", "spread"):
        loads[name].wait()

    z_copies = {}
    zu, zd, zo = zs[1], zs[3], zs[2]
    every, first, second = (0, 400), (0, 208), (208, 192)

    def z_go(slot, dy, rows, sem, to):
        where = at.at[slot, ys[dy], pl.ds(rows[0], rows[1]), :]
        z_copies[dy, sem] = go(copy(where, where, sz.at[dy, sem], rz.at[dy, sem], to, 0))

    def z_wait(dy, sem):
        wait(z_copies[dy, sem])

    def a_line(dy):
        for dx in range(4):
            d = (-dy % 4) * 4 + (-dx % 4)
            if d:
                wait(a_copies[d])
        line = ys[dy]
        for src in range(4):
            here = a_recv.at[line * 4 + src]
            top, low = slice(src * 32, src * 32 + 16), slice(src * 32 + 16, src * 32 + 32)
            tokens[top, 0:256] = here[:, 0:256]
            tokens[top, 256:384] = here[:, 512:640]
            tokens[low, 0:256] = here[:, 256:512]
            tokens[low, 384:512] = here[:, 512:640]
            tokens[top, 512:640] = here[:, 640:768]
            tokens[low, 512:640] = here[:, 768:896]
        at[z, line] = dot(pick[...], tokens[...], NT).astype(BF16)
        z_go(z, dy, every, 0, 1)
        z_go(z, dy, every, 1, 3)

    def z_relay(dy):
        z_wait(dy, 0)
        z_go(zd, dy, first, 2, 1)
        z_wait(dy, 1)
        z_go(zu, dy, second, 3, 3)

    def g_relay(j, da):
        for half in range(2):
            g_wait(half, 4 + 4 * j)
            g_go(half, near2(half, da, -1), upper, 6 + 4 * j, offset(half, 0, 1))
            g_wait(half, 5 + 4 * j)
            g_go(half, near2(half, da, 1), lower, 7 + 4 * j, offset(half, 0, -1))

    def regroup_w(src, dst):
        for q in range(PLANE):
            for zz in range(LINE):
                dst[q, 4 * zz:4 * zz + 4, :] = src[zz, 4 * q:4 * q + 4, :]

    def regroup_v(src, dst):
        for q in range(PLANE):
            for zz in range(LINE):
                dst[zz, 4 * q:4 * q + 4, :] = src[q, 4 * zz:4 * zz + 4, :]

    def plane_start(src, dst, ssem, rsem):
        out = []
        for d in far_first:
            to = inplane(d)
            out.append(go(copy(src.at[to], dst.at[me], ssem.at[d - 1], rsem.at[d - 1], 0, d)))
        dst[me] = src[me]
        return out

    def line_start(src, dst, ssem, rsem):
        out = {0: go(copy_across(src.at[z], dst.at[core, z], ssem.at[1, 0], rsem.at[1, 0]))}
        for d in (2, 1, 3):
            to = zs[d]
            out[d] = go(copy(src.at[to], dst.at[core, z], ssem.at[0, d], rsem.at[0, d], d, 0))
        dst[core, z] = src[z]
        return out

    def line_end(out, dst, ssem, rsem):
        forward = [out[0]]
        for d in (1, 3, 2):
            wait(out[d])
            where = dst.at[core, zs[-d % 4]]
            forward.append(go(copy_across(where, where, ssem.at[1, d], rsem.at[1, d])))
        return forward

    def apply_project(w):
        high, low = parts(w)
        return dot(project[0], high, NN) + dot(project[0], low, NN) + dot(project[1], high, NN)

    pm_copies, qm_copies, vm_copies = [], [], []

    def mean_kept(zz, q):
        return kept[0, zz, :, q * 128:(q + 1) * 128] + kept[1, q, :, zz * 128:(zz + 1) * 128]

    def own_part(ref, zz, q):
        lanes = pl.ds(pl.multiple_of((q + core * (zz - q)) * 128, 128), 128)
        return ref[zz + core * (q - zz), :, lanes]

    def momentum_step(which):
        if which == 1:
            for c in wm_copies:
                wait(c)
            regroup_w(wm_recv, pm_send)
            pm_copies.extend(plane_start(pm_send, pm_recv, spm, rpm))
        elif which == 2:
            for c in pm_copies:
                wait(c)
            qm_send[...] = apply_project(pm_recv[...].reshape(256, 128)).reshape(PLANE, 16, 128)
            qm_copies.extend(plane_start(qm_send, qm_recv, sqm, rqm))
        elif which == 3:
            for c in qm_copies:
                wait(c)
            regroup_v(qm_recv, vm)
            vm_copies.append(line_start(vm, vm_all, svm, rvm))
        else:
            for c in line_end(vm_copies[0], vm_all, svm, rvm):
                wait(c)
            for r in range(2):
                for zz in range(LINE):
                    high, low = parts(vm_all[r, zz])
                    kept[r, zz] = dot(jnp.concatenate([high, low, high], axis=0), expand[...], TN)[0:RBLOCKS]
            for zz in range(LINE):
                for q in range(4):
                    cols = slice(zz * ZCOLS + q * 128, zz * ZCOLS + (q + 1) * 128)
                    base_upd[:, cols] = F32(0.45) * mean_kept(zz, q)
                    base_new[:, cols] = F32(0.9) * (mom[:, cols].astype(F32) - own_part(kept.at[core], zz, q))

    def near_chunks():
        for half in range(2):
            g_wait(half, 0)
            g_go(half, near2(half, -1, 0), upper, 2, offset(half, 1, 0))
            g_wait(half, 1)
            g_go(half, near2(half, 1, 0), lower, 3, offset(half, -1, 0))
        for half in range(2):
            for j, da in ((1, -1), (2, 1)):
                g_go(half, near2(half, da, 0), whole, 4 + 4 * j, offset(half, 0, 1))
                g_go(half, near2(half, da, 0), whole, 5 + 4 * j, offset(half, 0, -1))

    def far_chunk():
        for half in range(2):
            g_wait(half, 2)
            g_wait(half, 3)
            g_go(half, near2(half, 2, 0), whole, 16, offset(half, 0, 1))
            g_go(half, near2(half, 2, 0), whole, 17, offset(half, 0, -1))

    for step in ORDER:
        kind, which = step[0], step[1:]
        if kind == "a":
            a_line(int(which))
        elif kind == "z":
            z_relay(int(which))
        elif kind == "s":
            near_chunks()
        elif kind == "f":
            far_chunk()
        elif kind == "m":
            momentum_step(int(which))
        else:
            g_relay(int(which), (0, -1, 1, 2)[int(which)])

    for j in range(4):
        for half in range(2):
            g_wait(half, 6 + 4 * j)
            g_wait(half, 7 + 4 * j)
    grad_copies = []

    def term(zz):
        left = jnp.concatenate([at[zz, yy] for yy in range(4)], axis=1)
        right = gt[:, :, pl.ds(pl.multiple_of(zz * ZTOK, ZTOK), ZTOK)]
        return dot(left, right.reshape(ZCOLS, ZTOK), NT)

    acc = term(z) + term(zd) + term(zu)
    for dy in (0, 1, 3, 2):
        z_wait(dy, 2)
        z_wait(dy, 3)
    acc = acc + term(zo)
    rows = acc[0:320]
    grad[...] = rows.reshape(LINE, RBLOCKS, ZCOLS)
    square = jnp.sum(jnp.sum(rows * rows, axis=0, keepdims=True), axis=1, keepdims=True)
    for d in range(1, 4):
        to = zs[d]
        grad_copies.append(go(copy(grad.at[to], grad_row.at[z], sgr.at[d - 1], rgr.at[d - 1], d, 0)))
    grad_row[z] = grad[z]
    mine = lax.broadcasted_iota(jnp.int32, (40, 128), 1) // 64 == core
    high, low = parts(acc[320:360] + acc[360:400])
    own = dot(high, twice[0], NT) + dot(low, twice[0], NT) + dot(high, twice[1], NT)
    coef[core, 0:40, :] = jnp.where(mine, own, F32(0.0))
    coef[core, 48:56, :] = jnp.where(mine[0:8], jnp.broadcast_to(square, (8, 128)), F32(0.0))
    share = go(copy_across(coef.at[core], coef.at[core], sfg.at[0], rfg.at[0]))
    v_copies = {}
    wait(share)
    high, low = parts(coef[0, 0:48] + coef[1, 0:48])
    result = dot(back[...], jnp.concatenate([high, low, high], axis=0), NN)
    sums = coef[0, 48:56] + coef[1, 48:56]
    row = lax.broadcasted_iota(jnp.int32, (8, 128), 0)
    vg[...] = result.reshape(64, 8, 128) + jnp.where(row == 5, sums, F32(0.0))[None]
    for dz, d in sorted(((dz, d) for dz in range(4) for d in range(16)), key=lambda v: -hops(*v)):
        if dz or d:
            to = zp_steps[dz] + yp_steps[d // 4] + xs[d % 4]
            v_copies[dz, d] = go(copy_to(
                vg.at[to], vg_all.at[t], sqg.at[dz, d], rqg.at[dz, d], (core, to)))
    vg_all[t] = vg[t]
    for step in MSTEPS:
        momentum_step(step)
    for c in v_copies.values():
        wait(c)

    square = jnp.sum(vg_all[:, 5:6, :], axis=0)
    factors = jnp.minimum(F32(1.0), 1.0 / jnp.sqrt(square / (RBLOCKS * BLOCK * COLS) + 1e-06))
    factor = jnp.where(core == 0, factors[:, 0:1], factors[:, 127:128])
    for src in range(64):
        zz, yy, xx = src // 16, src // 4 % 4, src % 4
        for r, line, i in ((0, zz, yy * 4 + xx), (1, yy, zz * 4 + xx)):
            top = line * RBLOCKS + OWN * i
            packed[r, top:top + OWN, :] = vg_all[src, 0:OWN, :]
    for r in range(2):
        high, low = parts(packed[r] * factors)
        result = dot(jnp.concatenate([high, low, high], axis=1), spread[r], NN)
        kept[r] = result.reshape(LINE, RBLOCKS, ZCOLS)
    for zz in range(LINE):
        for q in range(4):
            cols = slice(zz * ZCOLS + q * 128, zz * ZCOLS + (q + 1) * 128)
            upd_out[:, cols] = (base_upd[:, cols] + F32(0.5) * mean_kept(zz, q)).astype(BF16)
    for c in grad_copies:
        wait(c)
    for zz in range(LINE):
        for q in range(4):
            cols = slice(zz * ZCOLS + q * 128, zz * ZCOLS + (q + 1) * 128)
            more = factor * own_part(grad_row, zz, q) - own_part(kept.at[core], zz, q)
            new_out[:, cols] = (base_new[:, cols] + more).astype(BF16)
    for c in sent:
        if id(c) not in arrived:
            c.wait_recv()
        c.wait_send()


def body(activations, head_grads, momentum):
    dma = pltpu.SemaphoreType.DMA
    consts = [jnp.asarray(c) for c in tables()]
    vmem = pl.BlockSpec(memory_space=pltpu.VMEM)
    hbm = pl.BlockSpec(memory_space=pltpu.HBM)
    scratch = [
        pltpu.VMEM((32, RBLOCKS * BLOCK), BF16),
        pltpu.VMEM((32, TOKENS), BF16),
        pltpu.VMEM((RBLOCKS, COLS), BF16),
    ] + [pltpu.VMEM(c.shape[1:] if k in (0, 5) else c.shape, BF16) for k, c in enumerate(consts)] + [
        pltpu.VMEM((640, 256), BF16),
        pltpu.VMEM((2, 256, 384), BF16),
        pltpu.VMEM((PLANE, 16, 896), BF16),
        pltpu.VMEM((PLANE, 16, 896), BF16),
        pltpu.VMEM((128, 640), BF16),
        pltpu.VMEM((LINE, 4, ROWS, 128), BF16),
        pltpu.VMEM((PLANE, 32, TOKENS), BF16),
        pltpu.VMEM((LINE, RBLOCKS, ZCOLS), F32),
        pltpu.VMEM((LINE, RBLOCKS, ZCOLS), F32),
        pltpu.VMEM((LINE, 64, 128), F32),
        pltpu.VMEM((LINE, 64, 128), F32),
        pltpu.VMEM((PLANE, 16, 128), F32),
        pltpu.VMEM((PLANE, 16, 128), F32),
        pltpu.VMEM((PLANE, 16, 128), F32),
        pltpu.VMEM((PLANE, 16, 128), F32),
        pltpu.VMEM((LINE, 64, 128), F32),
        pltpu.VMEM((2, LINE, 64, 128), F32),
        pltpu.VMEM((2, 56, 128), F32),
        pltpu.VMEM((64, 8, 128), F32),
        pltpu.VMEM((64, 8, 128), F32),
        pltpu.VMEM((2, LINE * RBLOCKS, 128), F32),
        pltpu.VMEM((2, LINE, RBLOCKS, ZCOLS), F32),
        pltpu.VMEM((RBLOCKS, COLS), F32),
        pltpu.VMEM((RBLOCKS, COLS), F32),
        dma((11,)),
    ]
    for shape in ((15,), (4, 4), (2, 20), (3,), (3,), (15,), (15,), (2, 4), (4, 16), (1,)):
        scratch += [dma(shape), dma(shape)]
    new, upd = pl.pallas_call(
        kernel,
        out_shape=(
            pltpu.VMEM((RBLOCKS, COLS), BF16),
            pltpu.VMEM((RBLOCKS, COLS), BF16),
        ),
        in_specs=[hbm] * 11,
        out_specs=(vmem, vmem),
        scratch_shapes=scratch,
        compiler_params=pltpu.CompilerParams(
            collective_id=0, has_side_effects=True, vmem_limit_bytes=48 * 1024 * 1024
        ),
    )(*(pltpu.with_memory_space_constraint(v, pltpu.HBM)
        for v in (activations, head_grads.T, momentum.reshape(RBLOCKS, COLS), *consts)))

    def store(new_ref, upd_ref, new_hbm, upd_hbm, sems):
        copies = (
            pltpu.make_async_copy(new_ref, new_hbm, sems.at[0]),
            pltpu.make_async_copy(upd_ref, upd_hbm, sems.at[1]),
        )
        for c in copies:
            c.start()
        for c in copies:
            c.wait()

    new, upd = pl.pallas_call(
        store,
        out_shape=(
            jax.ShapeDtypeStruct((RBLOCKS, COLS), BF16),
            jax.ShapeDtypeStruct((RBLOCKS, COLS), BF16),
        ),
        in_specs=[vmem] * 2,
        out_specs=(hbm, hbm),
        scratch_shapes=[dma((2,))],
    )(*(pltpu.with_memory_space_constraint(v, pltpu.VMEM) for v in (new, upd)))
    return new[None, None], upd[None]


def solution(mesh):
    placed = (P(("dp", "tensor"), None), P("dp", "tensor"), P("dp", "tensor", None, None))
    return jax.shard_map(
        body,
        mesh=mesh,
        in_specs=placed,
        out_specs=(P("dp", "tensor", None, None), P("tensor", None, None)),
        check_vma=False,
    )
```

```python
import math

import jax
import jax.numpy as jnp
import ml_dtypes
import numpy as np
from jax import lax
from jax.experimental import pallas as pl
from jax.experimental.pallas import tpu as pltpu
from jax.sharding import PartitionSpec as P

BLOCK = 64
KEEP = 8
RBLOCKS = 80
COLS = 2048
TOKENS = 2048
LINE = 4
PLANE = 16
ZCOLS = COLS // LINE
ZTOK = TOKENS // LINE
OWN = 5
SHARE = 1024
ROWS = 400
MESH = pl.DeviceIdType.MESH
F32 = jnp.float32
BF16 = jnp.bfloat16
NT = (((1,), (1,)), ((), ()))
TN = (((0,), (0,)), ((), ()))
NN = (((1,), (0,)), ((), ()))
ORDER = ("a0", "s", "a1", "a3", "a2", "m1", "f", "z0", "g0", "g1", "g2", "z1", "m2", "g3", "z3", "z2", "m3")
START = "1A2"
MSTEPS = (4,)
AORD = (1, 3, 2, 4, 12, 5, 7, 13, 15, 6, 14, 8, 9, 11, 10)


def split(table):
    high = table.astype(np.float32).astype(ml_dtypes.bfloat16)
    low = (table - high.astype(np.float64)).astype(np.float32).astype(ml_dtypes.bfloat16)
    return high, low


def device(core, line, place):
    return line * 16 + place + core * (place // 4 * 16 + line * 4 + place % 4 - line * 16 - place)


def tables():
    k = np.arange(KEEP)[:, None]
    n = np.arange(BLOCK)[None, :]
    scale = np.where(k == 0, math.sqrt(1.0 / BLOCK), math.sqrt(2.0 / BLOCK))
    basis = scale * np.cos(math.pi * (2 * n + 1) * k / (2 * BLOCK))
    sort = np.zeros((2, 256, 256))
    for a in range(4):
        for z in range(LINE):
            for i in range(PLANE):
                for core in range(2):
                    sort[core, a * 64 + device(core, z, i), i * 16 + z * 4 + a] = 1
    pick = np.zeros((ROWS, 640))
    for tile in range(RBLOCKS // 4):
        for z in range(LINE):
            for a in range(4):
                lane = tile * 16 + z * 4 + a
                pick[z * RBLOCKS + 4 * tile + a, lane] = 1
                if tile >= 16:
                    pick[z * RBLOCKS + 4 * tile + a, lane + 192] = 1
    for k in range(OWN * KEEP):
        pick[320 + k, 512 + k] = 1
        pick[360 + k, 576 + k] = 1
    squeeze = np.zeros((2, 384, 128))
    for odd in range(2):
        for part, table in enumerate(split(basis)):
            for j in range(OWN):
                top = (j + odd) * BLOCK
                squeeze[odd, top:top + BLOCK, part * 64 + j * KEEP:part * 64 + (j + 1) * KEEP] = table.T.astype(np.float64)
    across = np.kron(np.eye(8), basis)
    across_h, across_l = split(across)
    twice = np.stack([np.concatenate([v, v], axis=0) for v in (across_h, across_l)])
    expand = np.concatenate([across_h, across_h, across_l], axis=0)
    project = []
    for core in range(2):
        order = np.array([device(core, z, i) for i in range(PLANE) for z in range(LINE)])
        project.append(np.stack(split(np.kron((basis.T @ basis)[np.ix_(order, order)], np.eye(4)))))
    back = np.zeros((BLOCK, 8, 48))
    for j in range(OWN):
        back[:, j, j * KEEP:(j + 1) * KEEP] = basis.T
    back_h, back_l = split(back.reshape(512, 48))
    back = np.concatenate([back_h, back_h, back_l], axis=1)
    spread = np.zeros((2, 2, 64, 512))
    for r in range(2):
        spread[r, r] = across
    spread_h, spread_l = split(spread.reshape(2, 128, 512))
    spread = np.concatenate([spread_h, spread_h, spread_l], axis=1)
    return (
        sort.astype(ml_dtypes.bfloat16),
        pick.astype(ml_dtypes.bfloat16),
        squeeze.astype(ml_dtypes.bfloat16),
        twice,
        expand,
        np.stack(project),
        back,
        spread,
    )


def dot(a, b, dims):
    return lax.dot_general(a, b, dims, preferred_element_type=F32)


def parts(x):
    high = x.astype(BF16)
    return high, (x - high.astype(F32)).astype(BF16)


def kernel(
    act_hbm, head_hbm, mom_hbm, sort_hbm, pick_hbm, squeeze_hbm, twice_hbm, expand_hbm, project_hbm, back_hbm, spread_hbm,
    new_out, upd_out,
    act, head, mom, sort, pick, squeeze, twice, expand, project, back, spread, stack, windows,
    a_send, a_recv, tokens, at, gt, grad, grad_row,
    wm_send, wm_recv, pm_send, pm_recv, qm_send, qm_recv, vm, vm_all,
    coef, vg, vg_all, packed, kept, base_new, base_upd,
    load, sa, ra, sz, rz, sg, rg, sgr, rgr, swm, rwm,
    spm, rpm, sqm, rqm, svm, rvm, sqg, rqg, sfg, rfg,
):
    core = lax.axis_index("dp")
    t = lax.axis_index("tensor")
    zp, yp, x = lax.div(t, 16), lax.rem(lax.div(t, 4), 4), lax.rem(t, 4)
    z, y = zp + core * (yp - zp), yp + core * (zp - yp)
    me = y * 4 + x

    def around(v):
        return [v] + [lax.rem(v + by, 4) for by in range(1, 4)]

    zs, ys, xs, zps, yps = around(z), around(y), around(x), around(zp), around(yp)
    z_steps = [v * (16 - 12 * core) for v in zs]
    y_steps = [v * (4 + 12 * core) for v in ys]
    y_slots = [v * 4 for v in ys]
    zp_steps, yp_steps = [v * 16 for v in zps], [v * 4 for v in yps]

    def inplane(d):
        return y_slots[d // 4] + xs[d % 4]

    def place(dz, d):
        return z_steps[dz % 4] + y_steps[d // 4] + xs[d % 4]

    def hops(dz, d):
        return sum(min(v, 4 - v) for v in (dz, d // 4, d % 4))

    far_first = sorted(range(1, 16), key=lambda d: -hops(0, d))

    def copy_to(src, dst, ssem, rsem, where):
        return pltpu.make_async_remote_copy(
            src_ref=src, dst_ref=dst, send_sem=ssem, recv_sem=rsem, device_id=where, device_id_type=MESH,
        )

    def copy(src, dst, ssem, rsem, dz, d):
        return copy_to(src, dst, ssem, rsem, (core, place(dz, d)))

    def copy_across(src, dst, ssem, rsem):
        return copy_to(src, dst, ssem, rsem, (1 - core, t))

    sent = []
    arrived = set()

    def go(c):
        c.start()
        sent.append(c)
        return c

    def wait(c):
        c.wait_recv()
        arrived.add(id(c))

    barrier = pltpu.get_barrier_semaphore()
    partners = [(core, place(0, d)) for d in far_first]
    partners += [(core, place(d, 0)) for d in (2, 1, 3)] + [(1 - core, t)]
    for where in partners:
        pl.semaphore_signal(barrier, inc=1, device_id=where, device_id_type=MESH)

    loads = {}
    for k, (name, src, dst) in enumerate((
        ("act", act_hbm, act), ("sort", sort_hbm.at[core], sort), ("squeeze", squeeze_hbm, squeeze), ("head", head_hbm, head),
        ("mom", mom_hbm, mom), ("pick", pick_hbm, pick), ("twice", twice_hbm, twice), ("expand", expand_hbm, expand),
        ("project", project_hbm.at[core], project), ("back", back_hbm, back), ("spread", spread_hbm, spread),
    )):
        loads[name] = pltpu.make_async_copy(src, dst, load.at[k])
        loads[name].start()
    loads["act"].wait()
    loads["sort"].wait()
    for tile in range(20):
        stack[tile * 32:(tile + 1) * 32, :] = act[:, tile * 256:(tile + 1) * 256]
    sorted_cols = dot(stack[...], sort[...], NN)
    group = lax.broadcasted_iota(jnp.int32, (32, 128), 1) // 16
    zero = jnp.zeros((32, 128), F32)
    for half in range(2):
        for octet in range(3):
            v = []
            for tile in range(octet * 8, octet * 8 + 8):
                if tile < 20:
                    v.append(sorted_cols[tile * 32:(tile + 1) * 32, half * 128:(half + 1) * 128])
                else:
                    v.append(zero)
            for d in (1, 2, 4):
                low = (group // d) % 2 == 0
                for k in range(8):
                    if k & d == 0:
                        a, b = v[k], v[k | d]
                        v[k] = jnp.where(low, a, pltpu.roll(b, 16 * d, 1))
                        v[k | d] = jnp.where(low, pltpu.roll(a, 128 - 16 * d, 1), b)
            for k in range(8):
                upper_rows, lower_rows = v[k][0:16], v[k][16:32]
                if octet < 2:
                    a_send[half * 8 + k, :, octet * 128:octet * 128 + 128] = upper_rows.astype(BF16)
                    a_send[half * 8 + k, :, octet * 128 + 256:octet * 128 + 384] = lower_rows.astype(BF16)
                else:
                    folded = jnp.where(group[0:16] < 4, upper_rows, pltpu.roll(lower_rows, 64, 1))
                    a_send[half * 8 + k, :, 512:640] = folded.astype(BF16)

    loads["squeeze"].wait()
    first_half = lax.broadcasted_iota(jnp.int32, (256, 128), 1) < 64
    for odd in range(2):
        for m in range(8):
            windows[odd, m * 32:(m + 1) * 32, :] = act[:, m * 640 + odd * 256:m * 640 + odd * 256 + 384]
        both = dot(windows[odd], squeeze[odd], NN)
        both = both + pltpu.roll(both, 64, 1)
        high = both.astype(BF16).astype(F32)
        both = jnp.where(first_half, high, both - high).astype(BF16)
        for m in range(8):
            a_send[2 * m + odd, :, 640:768] = both[m * 32:m * 32 + 16]
            a_send[2 * m + odd, :, 768:896] = both[m * 32 + 16:m * 32 + 32]

    loads["head"].wait()
    for tile in range(16):
        line, row = tile // 4, tile % 4
        lanes = pl.ds(pl.multiple_of((tile + core * (row * 4 + line - tile)) * 128, 128), 128)
        gt[me, :, tile * 128:(tile + 1) * 128] = head[:, lanes]

    pl.semaphore_wait(barrier, len(partners))


    def offset(half, da, db):
        return (db % 4 * 4 + da % 4) if half == 0 else (da % 4 * 4 + db % 4)

    def near2(half, da, db):
        return inplane(offset(half, da, db))

    g_copies = {}

    def g_go(half, slot, rows, sem, to):
        lanes = pl.ds(0, SHARE) if half == 0 else pl.ds(SHARE, TOKENS - SHARE)
        where = gt.at[slot, pl.ds(rows[0], rows[1]), lanes]
        g_copies[half, sem] = go(copy(where, where, sg.at[half, sem], rg.at[half, sem], 0, to))

    def g_wait(half, sem):
        wait(g_copies[half, sem])

    whole, upper, lower = (0, 32), (0, 16), (16, 16)

    a_copies = {}
    def start_a(offsets):
        for d in offsets:
            to = inplane(d)
            a_copies[d] = go(copy(a_send.at[to], a_recv.at[me], sa.at[d - 1], ra.at[d - 1], 0, d))

    def start_g1():
        for half in range(2):
            g_go(half, me, whole, 0, offset(half, 1, 0))
            g_go(half, me, whole, 1, offset(half, -1, 0))

    def start_g2():
        for half in range(2):
            g_go(half, me, whole, 4, offset(half, 0, 1))
            g_go(half, me, whole, 5, offset(half, 0, -1))


    a_recv[me] = a_send[me]
    tokens[...] = jnp.zeros_like(tokens)
    for step in START:
        {"A": lambda: start_a(AORD), "1": start_g1, "2": start_g2}[step]()

    def chunk(line, q):
        return pl.ds(pl.multiple_of((line * 4 + q + core * (q * 4 + line - line * 4 - q)) * 128, 128), 128)

    for name in ("mom", "twice"):
        loads[name].wait()
    wm_send[...] = jnp.zeros_like(wm_send)
    coef[core] = jnp.zeros((56, 128), F32)
    for zz in range(LINE):
        piece = jnp.concatenate([mom[:, chunk(zz, q)] for q in range(4)], axis=1)
        wm_send[zz, :, 0:RBLOCKS] = dot(twice[0, 0:64], piece, NT) + dot(twice[1, 0:64], piece, NT)
    wm_copies = []

    def wm_start():
        for d in range(1, 4):
            to = zs[d]
            wm_copies.append(go(copy(wm_send.at[to], wm_recv.at[z], swm.at[d - 1], rwm.at[d - 1], d, 0)))
        wm_recv[z] = wm_send[z]

    wm_start()

    for name in ("pick", "expand", "project", "back", "spread"):
        loads[name].wait()

    z_copies = {}
    zu, zd, zo = zs[1], zs[3], zs[2]
    every, first, second = (0, 400), (0, 208), (208, 192)

    def z_go(slot, dy, rows, sem, to):
        where = at.at[slot, ys[dy], pl.ds(rows[0], rows[1]), :]
        z_copies[dy, sem] = go(copy(where, where, sz.at[dy, sem], rz.at[dy, sem], to, 0))

    def z_wait(dy, sem):
        wait(z_copies[dy, sem])

    def a_line(dy):
        for dx in range(4):
            d = (-dy % 4) * 4 + (-dx % 4)
            if d:
                wait(a_copies[d])
        line = ys[dy]
        for src in range(4):
            here = a_recv.at[line * 4 + src]
            top, low = slice(src * 32, src * 32 + 16), slice(src * 32 + 16, src * 32 + 32)
            tokens[top, 0:256] = here[:, 0:256]
            tokens[top, 256:384] = here[:, 512:640]
            tokens[low, 0:256] = here[:, 256:512]
            tokens[low, 384:512] = here[:, 512:640]
            tokens[top, 512:640] = here[:, 640:768]
            tokens[low, 512:640] = here[:, 768:896]
        at[z, line] = dot(pick[...], tokens[...], NT).astype(BF16)
        z_go(z, dy, every, 0, 1)
        z_go(z, dy, every, 1, 3)

    def z_relay(dy):
        z_wait(dy, 0)
        z_go(zd, dy, first, 2, 1)
        z_wait(dy, 1)
        z_go(zu, dy, second, 3, 3)

    def g_relay(j, da):
        for half in range(2):
            g_wait(half, 4 + 4 * j)
            g_go(half, near2(half, da, -1), upper, 6 + 4 * j, offset(half, 0, 1))
            g_wait(half, 5 + 4 * j)
            g_go(half, near2(half, da, 1), lower, 7 + 4 * j, offset(half, 0, -1))

    def regroup_w(src, dst):
        for q in range(PLANE):
            for zz in range(LINE):
                dst[q, 4 * zz:4 * zz + 4, :] = src[zz, 4 * q:4 * q + 4, :]

    def regroup_v(src, dst):
        for q in range(PLANE):
            for zz in range(LINE):
                dst[zz, 4 * q:4 * q + 4, :] = src[q, 4 * zz:4 * zz + 4, :]

    def plane_start(src, dst, ssem, rsem):
        out = []
        for d in far_first:
            to = inplane(d)
            out.append(go(copy(src.at[to], dst.at[me], ssem.at[d - 1], rsem.at[d - 1], 0, d)))
        dst[me] = src[me]
        return out

    def line_start(src, dst, ssem, rsem):
        out = {0: go(copy_across(src.at[z], dst.at[core, z], ssem.at[1, 0], rsem.at[1, 0]))}
        for d in (2, 1, 3):
            to = zs[d]
            out[d] = go(copy(src.at[to], dst.at[core, z], ssem.at[0, d], rsem.at[0, d], d, 0))
        dst[core, z] = src[z]
        return out

    def line_end(out, dst, ssem, rsem):
        forward = [out[0]]
        for d in (1, 3, 2):
            wait(out[d])
            where = dst.at[core, zs[-d % 4]]
            forward.append(go(copy_across(where, where, ssem.at[1, d], rsem.at[1, d])))
        return forward

    def apply_project(w):
        high, low = parts(w)
        return dot(project[0], high, NN) + dot(project[0], low, NN) + dot(project[1], high, NN)

    pm_copies, qm_copies, vm_copies = [], [], []

    def mean_kept(zz, q):
        return kept[0, zz, :, q * 128:(q + 1) * 128] + kept[1, q, :, zz * 128:(zz + 1) * 128]

    def own_part(ref, zz, q):
        lanes = pl.ds(pl.multiple_of((q + core * (zz - q)) * 128, 128), 128)
        return ref[zz + core * (q - zz), :, lanes]

    def momentum_step(which):
        if which == 1:
            for c in wm_copies:
                wait(c)
            regroup_w(wm_recv, pm_send)
            pm_copies.extend(plane_start(pm_send, pm_recv, spm, rpm))
        elif which == 2:
            for c in pm_copies:
                wait(c)
            qm_send[...] = apply_project(pm_recv[...].reshape(256, 128)).reshape(PLANE, 16, 128)
            qm_copies.extend(plane_start(qm_send, qm_recv, sqm, rqm))
        elif which == 3:
            for c in qm_copies:
                wait(c)
            regroup_v(qm_recv, vm)
            vm_copies.append(line_start(vm, vm_all, svm, rvm))
        else:
            for c in line_end(vm_copies[0], vm_all, svm, rvm):
                wait(c)
            for r in range(2):
                for zz in range(LINE):
                    high, low = parts(vm_all[r, zz])
                    kept[r, zz] = dot(jnp.concatenate([high, low, high], axis=0), expand[...], TN)[0:RBLOCKS]
            for zz in range(LINE):
                for q in range(4):
                    cols = slice(zz * ZCOLS + q * 128, zz * ZCOLS + (q + 1) * 128)
                    base_upd[:, cols] = F32(0.45) * mean_kept(zz, q)
                    base_new[:, cols] = F32(0.9) * (mom[:, cols].astype(F32) - own_part(kept.at[core], zz, q))

    def near_chunks():
        for half in range(2):
            g_wait(half, 0)
            g_go(half, near2(half, -1, 0), upper, 2, offset(half, 1, 0))
            g_wait(half, 1)
            g_go(half, near2(half, 1, 0), lower, 3, offset(half, -1, 0))
        for half in range(2):
            for j, da in ((1, -1), (2, 1)):
                g_go(half, near2(half, da, 0), whole, 4 + 4 * j, offset(half, 0, 1))
                g_go(half, near2(half, da, 0), whole, 5 + 4 * j, offset(half, 0, -1))

    def far_chunk():
        for half in range(2):
            g_wait(half, 2)
            g_wait(half, 3)
            g_go(half, near2(half, 2, 0), whole, 16, offset(half, 0, 1))
            g_go(half, near2(half, 2, 0), whole, 17, offset(half, 0, -1))

    for step in ORDER:
        kind, which = step[0], step[1:]
        if kind == "a":
            a_line(int(which))
        elif kind == "z":
            z_relay(int(which))
        elif kind == "s":
            near_chunks()
        elif kind == "f":
            far_chunk()
        elif kind == "m":
            momentum_step(int(which))
        else:
            g_relay(int(which), (0, -1, 1, 2)[int(which)])

    for j in range(4):
        for half in range(2):
            g_wait(half, 6 + 4 * j)
            g_wait(half, 7 + 4 * j)
    grad_copies = []

    def term(zz):
        left = jnp.concatenate([at[zz, yy] for yy in range(4)], axis=1)
        right = gt[:, :, pl.ds(pl.multiple_of(zz * ZTOK, ZTOK), ZTOK)]
        return dot(left, right.reshape(ZCOLS, ZTOK), NT)

    acc = term(z) + term(zd) + term(zu)
    for dy in (0, 1, 3, 2):
        z_wait(dy, 2)
        z_wait(dy, 3)
    acc = acc + term(zo)
    rows = acc[0:320]
    grad[...] = rows.reshape(LINE, RBLOCKS, ZCOLS)
    square = jnp.sum(jnp.sum(rows * rows, axis=0, keepdims=True), axis=1, keepdims=True)
    for d in range(1, 4):
        to = zs[d]
        grad_copies.append(go(copy(grad.at[to], grad_row.at[z], sgr.at[d - 1], rgr.at[d - 1], d, 0)))
    grad_row[z] = grad[z]
    mine = lax.broadcasted_iota(jnp.int32, (40, 128), 1) // 64 == core
    high, low = parts(acc[320:360] + acc[360:400])
    own = dot(high, twice[0], NT) + dot(low, twice[0], NT) + dot(high, twice[1], NT)
    coef[core, 0:40, :] = jnp.where(mine, own, F32(0.0))
    coef[core, 48:56, :] = jnp.where(mine[0:8], jnp.broadcast_to(square, (8, 128)), F32(0.0))
    share = go(copy_across(coef.at[core], coef.at[core], sfg.at[0], rfg.at[0]))
    v_copies = {}
    wait(share)
    high, low = parts(coef[0, 0:48] + coef[1, 0:48])
    result = dot(back[...], jnp.concatenate([high, low, high], axis=0), NN)
    sums = coef[0, 48:56] + coef[1, 48:56]
    row = lax.broadcasted_iota(jnp.int32, (8, 128), 0)
    vg[...] = result.reshape(64, 8, 128) + jnp.where(row == 5, sums, F32(0.0))[None]
    for dz, d in sorted(((dz, d) for dz in range(4) for d in range(16)), key=lambda v: -hops(*v)):
        if dz or d:
            to = zp_steps[dz] + yp_steps[d // 4] + xs[d % 4]
            v_copies[dz, d] = go(copy_to(
                vg.at[to], vg_all.at[t], sqg.at[dz, d], rqg.at[dz, d], (core, to)))
    vg_all[t] = vg[t]
    for step in MSTEPS:
        momentum_step(step)
    for c in v_copies.values():
        wait(c)

    square = jnp.sum(vg_all[:, 5:6, :], axis=0)
    factors = jnp.minimum(F32(1.0), 1.0 / jnp.sqrt(square / (RBLOCKS * BLOCK * COLS) + 1e-06))
    factor = jnp.where(core == 0, factors[:, 0:1], factors[:, 127:128])
    for src in range(64):
        zz, yy, xx = src // 16, src // 4 % 4, src % 4
        for r, line, i in ((0, zz, yy * 4 + xx), (1, yy, zz * 4 + xx)):
            top = line * RBLOCKS + OWN * i
            packed[r, top:top + OWN, :] = vg_all[src, 0:OWN, :]
    for r in range(2):
        high, low = parts(packed[r] * factors)
        result = dot(jnp.concatenate([high, low, high], axis=1), spread[r], NN)
        kept[r] = result.reshape(LINE, RBLOCKS, ZCOLS)
    for zz in range(LINE):
        for q in range(4):
            cols = slice(zz * ZCOLS + q * 128, zz * ZCOLS + (q + 1) * 128)
            upd_out[:, cols] = (base_upd[:, cols] + F32(0.5) * mean_kept(zz, q)).astype(BF16)
            base_new[:, cols] = base_new[:, cols] - own_part(kept.at[core], zz, q)
    for c in grad_copies:
        wait(c)
    for zz in range(LINE):
        for q in range(4):
            cols = slice(zz * ZCOLS + q * 128, zz * ZCOLS + (q + 1) * 128)
            new_out[:, cols] = (base_new[:, cols] + factor * own_part(grad_row, zz, q)).astype(BF16)
    for c in sent:
        if id(c) not in arrived:
            c.wait_recv()
        c.wait_send()


def body(activations, head_grads, momentum):
    dma = pltpu.SemaphoreType.DMA
    consts = [jnp.asarray(c) for c in tables()]
    vmem = pl.BlockSpec(memory_space=pltpu.VMEM)
    hbm = pl.BlockSpec(memory_space=pltpu.HBM)
    scratch = [
        pltpu.VMEM((32, RBLOCKS * BLOCK), BF16),
        pltpu.VMEM((32, TOKENS), BF16),
        pltpu.VMEM((RBLOCKS, COLS), BF16),
    ] + [pltpu.VMEM(c.shape[1:] if k in (0, 5) else c.shape, BF16) for k, c in enumerate(consts)] + [
        pltpu.VMEM((640, 256), BF16),
        pltpu.VMEM((2, 256, 384), BF16),
        pltpu.VMEM((PLANE, 16, 896), BF16),
        pltpu.VMEM((PLANE, 16, 896), BF16),
        pltpu.VMEM((128, 640), BF16),
        pltpu.VMEM((LINE, 4, ROWS, 128), BF16),
        pltpu.VMEM((PLANE, 32, TOKENS), BF16),
        pltpu.VMEM((LINE, RBLOCKS, ZCOLS), F32),
        pltpu.VMEM((LINE, RBLOCKS, ZCOLS), F32),
        pltpu.VMEM((LINE, 64, 128), F32),
        pltpu.VMEM((LINE, 64, 128), F32),
        pltpu.VMEM((PLANE, 16, 128), F32),
        pltpu.VMEM((PLANE, 16, 128), F32),
        pltpu.VMEM((PLANE, 16, 128), F32),
        pltpu.VMEM((PLANE, 16, 128), F32),
        pltpu.VMEM((LINE, 64, 128), F32),
        pltpu.VMEM((2, LINE, 64, 128), F32),
        pltpu.VMEM((2, 56, 128), F32),
        pltpu.VMEM((64, 8, 128), F32),
        pltpu.VMEM((64, 8, 128), F32),
        pltpu.VMEM((2, LINE * RBLOCKS, 128), F32),
        pltpu.VMEM((2, LINE, RBLOCKS, ZCOLS), F32),
        pltpu.VMEM((RBLOCKS, COLS), F32),
        pltpu.VMEM((RBLOCKS, COLS), F32),
        dma((11,)),
    ]
    for shape in ((15,), (4, 4), (2, 20), (3,), (3,), (15,), (15,), (2, 4), (4, 16), (1,)):
        scratch += [dma(shape), dma(shape)]
    new, upd = pl.pallas_call(
        kernel,
        out_shape=(
            pltpu.VMEM((RBLOCKS, COLS), BF16),
            pltpu.VMEM((RBLOCKS, COLS), BF16),
        ),
        in_specs=[hbm] * 11,
        out_specs=(vmem, vmem),
        scratch_shapes=scratch,
        compiler_params=pltpu.CompilerParams(
            collective_id=0, has_side_effects=True, vmem_limit_bytes=48 * 1024 * 1024
        ),
    )(*(pltpu.with_memory_space_constraint(v, pltpu.HBM)
        for v in (activations, head_grads.T, momentum.reshape(RBLOCKS, COLS), *consts)))

    def store(new_ref, upd_ref, new_hbm, upd_hbm, sems):
        copies = (
            pltpu.make_async_copy(new_ref, new_hbm, sems.at[0]),
            pltpu.make_async_copy(upd_ref, upd_hbm, sems.at[1]),
        )
        for c in copies:
            c.start()
        for c in copies:
            c.wait()

    new, upd = pl.pallas_call(
        store,
        out_shape=(
            jax.ShapeDtypeStruct((RBLOCKS, COLS), BF16),
            jax.ShapeDtypeStruct((RBLOCKS, COLS), BF16),
        ),
        in_specs=[vmem] * 2,
        out_specs=(hbm, hbm),
        scratch_shapes=[dma((2,))],
    )(*(pltpu.with_memory_space_constraint(v, pltpu.VMEM) for v in (new, upd)))
    return new[None, None], upd[None]


def solution(mesh):
    placed = (P(("dp", "tensor"), None), P("dp", "tensor"), P("dp", "tensor", None, None))
    return jax.shard_map(
        body,
        mesh=mesh,
        in_specs=placed,
        out_specs=(P("dp", "tensor", None, None), P("tensor", None, None)),
        check_vma=False,
    )
```
